32 devices in a mesh: ma: 16 (over z, x, core), bl: 2 (over y).
Axes of the slice: x: 2, y: 2, z: 4, core: 2. Of those that a mesh axis runs over, the one named last changes fastest.
Arguments:
- visibilities: bfloat16 [2, 4160, 8192], P(None, 'bl', 'ma'), may hold values from -6 to 6
- beam_blocks: bfloat16 [16, 2, 4160, 1000], P('ma', None, 'bl'), may hold values from -0.125 to 0.125
- feed_pairs: int32 [4160, 2], P('bl'), may hold values from 0 to 1023
- feed_gains: float32 [2, 1024], replicated, may hold values from -1.5 to 1.5
- m_order: int32 [16], replicated, may hold values from 0 to 15, each once
Outputs:
- sky_modes: float32 [2, 16, 1000], P(None, 'ma', 'bl')
The draws below stay inside these ranges and needn't reach their ends.
All inputs are finite; a program needn't handle non-finite values.
Results may differ from the reference program's by a relative error of at most 0.0049.
Values may be sent and summed in bfloat16 or wider, within the bound.
A program may use at most 64 MiB of HBM per device.

```python
import jax
import jax.numpy as jnp
from jax import lax

NT = 8192
L = 1000
NFEED = 1024
NB = 4160
M = 16


def with_ends(values, key, low, top_value):
    place = [jax.random.randint(jax.random.fold_in(key, axis), (), 0, length) for axis, length in enumerate(values.shape)]
    main_axis = values.shape.index(max(values.shape))
    neighbour = place[:main_axis] + [(place[main_axis] + 1) % values.shape[main_axis]] + place[main_axis + 1:]
    return values.at[tuple(place)].set(low).at[tuple(neighbour)].set(top_value)


def with_spikes(drawn, rng, source, target, shards_of, factor):
    def block_of(position):
        return (jnp.arange(drawn.shape[position]) // (drawn.shape[position] // shards_of)).reshape((-1,) + (1,) * (drawn.ndim - 1 - position))

    near = jax.random.permutation(rng, shards_of)[block_of(target)]
    other_side = (block_of(target) + shards_of // 2) % shards_of
    return jnp.where((block_of(source) == near) | (block_of(source) == other_side), factor * drawn, drawn)


def block_levels(own_key, extent, cuts, smallest, high):
    loudness = 1.0
    for position, shards_of in cuts:
        draws = jax.random.uniform(jax.random.fold_in(jax.random.fold_in(own_key, 6), position), (shards_of,), jnp.float32, smallest / len(cuts), high / len(cuts))
        loudness = loudness * jnp.repeat(jnp.exp(draws), extent[position] // shards_of).reshape((-1,) + (1,) * (len(extent) - 1 - position))
    return loudness


def centred(own_key, shape, spread, reach, split=(), kind=jnp.bfloat16):
    array = jax.random.normal(own_key, shape, jnp.float32) * spread
    if len(split) > 0:
        array = block_levels(own_key, shape, split, -0.22, 0.18) * array
    return jnp.clip(array, min=-reach, max=reach).astype(kind)


def noise_with(key, dims, scale, most, pieces, heavy, kind=jnp.bfloat16):
    values = scale * jax.random.normal(key, dims, jnp.float32)
    if pieces:
        values = values * block_levels(key, dims, pieces, -0.22, 0.18)
    return jnp.clip(with_spikes(values, jax.random.fold_in(key, 3), *heavy), -most, most).astype(kind)


def setup_inputs(seed: int = 0) -> dict:
    keys = jax.random.split(jax.random.key(seed), 6)
    visibilities = centred(keys[0], (2, NB, NT), 1.0, 6.0, ((1, 2), (2, 16)))
    beam_blocks = noise_with(keys[1], (M, 2, NB, L), NB ** -0.5, 0.125, ((0, 16), (2, 2)), (2, 3, 2, 2.0))
    feed_pairs = with_ends(jax.random.randint(keys[2], (NB, 2), 0, NFEED), jax.random.fold_in(keys[2], 1), 0, NFEED - 1).astype(jnp.int32)
    feed_gains = jnp.clip(jax.random.uniform(keys[3], (2, NFEED), jnp.float32, -1.5, 1.5), -1.5, 1.5)
    m_order = jax.random.permutation(keys[4], M).astype(jnp.int32)
    return dict(visibilities=visibilities, beam_blocks=beam_blocks, feed_pairs=feed_pairs, feed_gains=feed_gains, m_order=m_order)


def dft_weights(time_index, m_values):
    wrapped = jnp.mod(time_index[:, None] * m_values[None, :], NT).astype(jnp.float32)
    phases = wrapped * (2.0 * jnp.pi / NT)
    scale = 1.0 / jnp.sqrt(jnp.float32(NT))
    cos_part = (jnp.cos(phases) * scale).astype(jnp.bfloat16)
    sin_part = (jnp.sin(phases) * scale).astype(jnp.bfloat16)
    upper = jnp.concatenate([cos_part, -sin_part], axis=1)
    lower = jnp.concatenate([sin_part, cos_part], axis=1)
    return jnp.concatenate([upper, lower], axis=0)

def reference(visibilities, beam_blocks, feed_pairs, feed_gains, m_order):
    count = m_order.shape[0]
    m_values = (m_order - count // 2).astype(jnp.int32)
    time_index = jnp.arange(NT, dtype=jnp.int32)
    weights = dft_weights(time_index, m_values)
    stacked_in = jnp.concatenate([visibilities[0], visibilities[1]], axis=1)
    spectra_flat = jnp.dot(stacked_in, weights, preferred_element_type=jnp.float32)
    spectra = jnp.stack([spectra_flat[:, :count], spectra_flat[:, count:]]).astype(jnp.bfloat16)
    first_feed = feed_pairs[:, 0]
    second_feed = feed_pairs[:, 1]
    gain_re = feed_gains[0]
    gain_im = feed_gains[1]
    a_re = gain_re[first_feed]
    a_im = gain_im[first_feed]
    b_re = gain_re[second_feed]
    b_im = gain_im[second_feed]
    factor_re = (a_re * b_re + a_im * b_im)[:, None]
    factor_im = (a_im * b_re - a_re * b_im)[:, None]
    spec_re = spectra[0].astype(jnp.float32)
    spec_im = spectra[1].astype(jnp.float32)
    weighted_re = (spec_re * factor_re - spec_im * factor_im).astype(jnp.bfloat16)
    weighted_im = (spec_re * factor_im + spec_im * factor_re).astype(jnp.bfloat16)
    row_real = jnp.concatenate([weighted_re, weighted_im], axis=0)
    row_imag = jnp.concatenate([weighted_im, -weighted_re], axis=0)
    vectors = jnp.stack([row_real, row_imag])
    vectors = jnp.transpose(vectors, (2, 0, 1))
    total_rows = beam_blocks.shape[2]
    width = beam_blocks.shape[3]

    def project(pair):
        vector, block = pair
        flat_block = block.reshape(2 * total_rows, width)
        return jnp.dot(vector, flat_block, preferred_element_type=jnp.float32)
    result = lax.map(project, (vectors, beam_blocks))
    return jnp.transpose(result, (1, 0, 2))
```

```python
import functools

import jax
import jax.numpy as jnp
import numpy as np
from jax import lax
from jax.experimental import pallas as pl
from jax.experimental.pallas import tpu as pltpu
from jax.sharding import PartitionSpec as P

NT = 8192
LANES = 128
CHUNKS = 2
MESH = pl.DeviceIdType.MESH


def trig(k):
    quarter = NT // 4
    turn = (k + quarter // 2) // quarter
    x = (k - turn * quarter).astype(jnp.float32) * np.float32(2.0 * np.pi / NT)
    y = x * x
    sin_x = x * (1.0 + y * (-1.0 / 6 + y * (1.0 / 120 + y * (-1.0 / 5040 + y * (1.0 / 362880)))))
    cos_x = 1.0 + y * (-0.5 + y * (1.0 / 24 + y * (-1.0 / 720 + y * (1.0 / 40320))))
    odd = (turn & 1) == 1
    cos_k = jnp.where(odd, sin_x, cos_x)
    sin_k = jnp.where(odd, cos_x, sin_x)
    cos_k = jnp.where(((turn + 1) & 2) == 2, -cos_k, cos_k)
    sin_k = jnp.where((turn & 2) == 2, -sin_k, sin_k)
    return cos_k, sin_k


def peer_order(count):
    return sorted(range(1, count), key=lambda k: abs(k - count // 2))


def kernel(
    n_ma, n_bl, vis, beam, pairs, gains, order, out,
    vis_v, beam_v, pairs_v, gains_v, order_s,
    sums, part, got, rem_part, rem_got, table, factor, lhs, share, share_got,
    vis_sem, beam_sem, small_sem, send_sem, recv_sem, rem_send, rem_recv, bl_send, bl_recv,
):
    me = lax.axis_index("ma")
    my_bl = lax.axis_index("bl")
    rows = vis.shape[1]
    local_times = vis.shape[2]
    cols = rows // LANES
    rem = rows - cols * LANES
    per = cols // CHUNKS
    peers = [lax.rem(me + k, n_ma) for k in range(n_ma)]
    order_of = peer_order(n_ma)

    barrier = pltpu.get_barrier_semaphore()
    for k in range(1, n_ma):
        pl.semaphore_signal(barrier, inc=1, device_id={"ma": peers[k]}, device_id_type=MESH)
    bl_peers = [lax.rem(my_bl + k, n_bl) for k in range(n_bl)]
    for k in range(1, n_bl):
        pl.semaphore_signal(barrier, inc=1, device_id={"bl": bl_peers[k]}, device_id_type=MESH)

    order_copy = pltpu.make_async_copy(order, order_s, small_sem.at[0])
    order_copy.start()
    starts = [c * per * LANES for c in range(CHUNKS)]
    sizes = [per * LANES] * (CHUNKS - 1) + [per * LANES + rem]
    vis_copies = []
    for c in range(CHUNKS):
        pieces = []
        for p in range(2):
            piece = pl.ds(starts[c], sizes[c])
            copy = pltpu.make_async_copy(vis.at[p, piece], vis_v.at[p, piece], vis_sem.at[c, p])
            copy.start()
            pieces.append(copy)
        vis_copies.append(pieces)
    pairs_copy = pltpu.make_async_copy(pairs, pairs_v, small_sem.at[1])
    pairs_copy.start()
    gains_copy = pltpu.make_async_copy(gains, gains_v, small_sem.at[2])
    gains_copy.start()
    beam_copies = []
    for c in range(CHUNKS):
        pieces = []
        for p in range(2):
            piece = pl.ds(starts[c], sizes[c])
            pieces.append(pltpu.make_async_copy(beam.at[0, p, piece], beam_v.at[p, piece], beam_sem.at[c, p]))
        beam_copies.append(pieces)

    order_copy.wait()
    slot = lax.broadcasted_iota(jnp.int32, (n_ma, LANES), 0)
    m_value = jnp.zeros((n_ma, LANES), jnp.int32)
    for j in range(n_ma):
        m_value = jnp.where(slot == j, order_s[j] - n_ma // 2, m_value)
    left, right = [], []
    for block in range(local_times // LANES):
        time = me * local_times + block * LANES + lax.broadcasted_iota(jnp.int32, (n_ma, LANES), 1)
        cos_k, sin_k = trig((time * m_value) & (NT - 1))
        scale = np.float32(1.0 / np.sqrt(np.float32(NT)))
        cos_k, sin_k = cos_k * scale, sin_k * scale
        left.append(jnp.concatenate([cos_k, -sin_k], axis=0).astype(jnp.bfloat16))
        right.append(jnp.concatenate([sin_k, cos_k], axis=0).astype(jnp.bfloat16))
    left = jnp.concatenate(left, axis=1)
    right = jnp.concatenate(right, axis=1)

    def transform(start, size):
        contract = (((1,), (1,)), ((), ()))
        re = lax.dot_general(left, vis_v[0, start:start + size, :], contract, preferred_element_type=jnp.float32)
        im = lax.dot_general(right, vis_v[1, start:start + size, :], contract, preferred_element_type=jnp.float32)
        return re + im

    sends = []
    for c in range(CHUNKS):
        for copy in vis_copies[c]:
            copy.wait()
        if c == CHUNKS - 1:
            for pieces in beam_copies:
                for copy in pieces:
                    copy.start()
        step = 2
        for i in range(0, per, step):
            flat = transform(starts[c] + i * LANES, step * LANES)
            for u in range(step):
                for p in range(2):
                    sums[c, pl.ds(p * per + i + u, n_ma, stride=2 * per), :] = (
                        flat[p * n_ma:(p + 1) * n_ma, u * LANES:(u + 1) * LANES]
                    )
        part[c] = sums[c].astype(jnp.bfloat16).reshape(n_ma, 2 * per, LANES)
        if c == 0:
            pl.semaphore_wait(barrier, n_ma - 1 + n_bl - 1)
        for k in order_of:
            copy = pltpu.make_async_remote_copy(
                src_ref=part.at[c, peers[k]], dst_ref=got.at[c, me],
                send_sem=send_sem.at[c, k], recv_sem=recv_sem.at[c, k],
                device_id={"ma": peers[k]}, device_id_type=MESH,
            )
            copy.start()
            sends.append((c, k, copy))
    flat = transform(cols * LANES, rem)
    wide = jnp.concatenate(
        [flat[:n_ma], flat[n_ma:], jnp.zeros((n_ma, LANES - 2 * rem), jnp.float32)], axis=1
    )
    for j in range(n_ma):
        rem_part[j] = wide[j:j + 1, :]
    for k in order_of:
        copy = pltpu.make_async_remote_copy(
            src_ref=rem_part.at[peers[k]], dst_ref=rem_got.at[me],
            send_sem=rem_send.at[k], recv_sem=rem_recv.at[k],
            device_id={"ma": peers[k]}, device_id_type=MESH,
        )
        copy.start()
        sends.append((CHUNKS, k, copy))

    pairs_copy.wait()
    gains_copy.wait()
    high = gains.shape[1] // LANES
    for comp in range(2):
        for h in range(high):
            table[comp * high + h:comp * high + h + 1, :] = gains_v[comp:comp + 1, h * LANES:(h + 1) * LANES]
    whole = table[...]
    first = whole.astype(jnp.bfloat16)
    rest = whole - first.astype(jnp.float32)
    second = rest.astype(jnp.bfloat16)
    third = (rest - second.astype(jnp.float32)).astype(jnp.bfloat16)
    thirds = jnp.concatenate([first, second, third], axis=0)

    def gain_of(feed, start, size):
        index = pairs_v[feed:feed + 1, start:start + size]
        low = lax.broadcasted_iota(jnp.int32, (LANES, size), 0)
        hot = jnp.where(low == (index & (LANES - 1)), 1.0, 0.0).astype(jnp.bfloat16)
        picked = jnp.dot(thirds, hot, preferred_element_type=jnp.float32)
        picked = picked[:2 * high] + picked[2 * high:4 * high] + picked[4 * high:]
        mask = lax.broadcasted_iota(jnp.int32, (high, size), 0) == index // LANES
        re = jnp.sum(jnp.where(mask, picked[:high], 0.0), axis=0, keepdims=True)
        im = jnp.sum(jnp.where(mask, picked[high:], 0.0), axis=0, keepdims=True)
        return re, im

    def factor_of(start, size):
        a_re, a_im = gain_of(0, start, size)
        b_re, b_im = gain_of(1, start, size)
        return a_re * b_re + a_im * b_im, a_im * b_re - a_re * b_im

    for i in range(0, cols, 2):
        f_re, f_im = factor_of(i * LANES, 2 * LANES)
        for u in range(2):
            factor[0, i + u:i + u + 1, :] = f_re[:, u * LANES:(u + 1) * LANES]
            factor[1, i + u:i + u + 1, :] = f_im[:, u * LANES:(u + 1) * LANES]
    rem_re, rem_im = factor_of(cols * LANES, rem)

    def weigh(s_re, s_im, f_re, f_im):
        s_re = s_re.astype(jnp.bfloat16).astype(jnp.float32)
        s_im = s_im.astype(jnp.bfloat16).astype(jnp.float32)
        return s_re * f_re - s_im * f_im, s_re * f_im + s_im * f_re

    total = None
    for c in range(CHUNKS):
        for copy in beam_copies[c]:
            copy.wait()
        mine = pl.multiple_of(me * 2 * per, 2 * per)
        spectra = sums[c, pl.ds(mine, 2 * per), :]
        for which, k, copy in sends:
            if which == c:
                copy.wait_recv()
        for k in range(1, n_ma):
            spectra = spectra + got[c, peers[k]].astype(jnp.float32)
        w_re, w_im = weigh(
            spectra[:per], spectra[per:], factor[0, c * per:(c + 1) * per], factor[1, c * per:(c + 1) * per]
        )
        for i in range(per):
            at = slice(starts[c] + i * LANES, starts[c] + (i + 1) * LANES)
            lhs[0:1, at] = w_re[i:i + 1]
            lhs[1:2, at] = w_im[i:i + 1]
        if c == CHUNKS - 1:
            for which, k, copy in sends:
                if which == CHUNKS:
                    copy.wait_recv()
            tail = rem_part[me]
            for k in range(1, n_ma):
                tail = tail + rem_got[peers[k]]
            w_re, w_im = weigh(tail[:, :rem], tail[:, rem:2 * rem], rem_re, rem_im)
            lhs[0:1, cols * LANES:rows] = w_re
            lhs[1:2, cols * LANES:rows] = w_im
        at = slice(starts[c], starts[c] + sizes[c])
        w_re, w_im = lhs[0:1, at], lhs[1:2, at]
        row_a = jnp.concatenate([w_re, w_im], axis=0).astype(jnp.bfloat16)
        row_b = jnp.concatenate([w_im, -w_re], axis=0).astype(jnp.bfloat16)
        term = jnp.dot(row_a, beam_v[0, at, :], preferred_element_type=jnp.float32)
        term = term + jnp.dot(row_b, beam_v[1, at, :], preferred_element_type=jnp.float32)
        total = term if total is None else total + term

    width = out.shape[2]
    for d in range(n_bl):
        share[d, :, 0:width] = total[:, d * width:(d + 1) * width]
    bl_copies = []
    for k in range(1, n_bl):
        copy = pltpu.make_async_remote_copy(
            src_ref=share.at[bl_peers[k]], dst_ref=share_got.at[my_bl],
            send_sem=bl_send.at[k], recv_sem=bl_recv.at[k],
            device_id={"bl": bl_peers[k]}, device_id_type=MESH,
        )
        copy.start()
        bl_copies.append(copy)
    for which, k, copy in sends:
        copy.wait_send()
    result = share[my_bl]
    for k in range(1, n_bl):
        bl_copies[k - 1].wait_recv()
    for k in range(1, n_bl):
        result = result + share_got[bl_peers[k]]
    out[:, 0, :] = result[:, :width]
    for copy in bl_copies:
        copy.wait_send()


def per_device(n_ma, n_bl, visibilities, beam_blocks, feed_pairs, feed_gains, m_order):
    _, rows, local_times = visibilities.shape
    width = beam_blocks.shape[3]
    assert m_order.shape[0] == n_ma and beam_blocks.shape[0] == 1
    cols = rows // LANES
    rem = rows - cols * LANES
    per = cols // CHUNKS
    assert cols % (2 * CHUNKS) == 0 and (2 * per) % 16 == 0 and 0 < 2 * rem <= LANES
    share_width = width // n_bl
    share_pad = -(-share_width // LANES) * LANES
    feeds = feed_gains.shape[1]
    f32, bf16 = jnp.float32, jnp.bfloat16
    dma = pltpu.SemaphoreType.DMA
    return pl.pallas_call(
        functools.partial(kernel, n_ma, n_bl),
        out_shape=jax.ShapeDtypeStruct((2, 1, share_width), f32),
        in_specs=[pl.BlockSpec(memory_space=pl.ANY)] * 5,
        out_specs=pl.BlockSpec(memory_space=pltpu.VMEM),
        scratch_shapes=[
            pltpu.VMEM((2, rows, local_times), bf16),
            pltpu.VMEM((2, rows, width), bf16),
            pltpu.VMEM((2, rows), jnp.int32),
            pltpu.VMEM((2, feeds), f32),
            pltpu.SMEM((n_ma,), jnp.int32),
            pltpu.VMEM((CHUNKS, n_ma * 2 * per, LANES), f32),
            pltpu.VMEM((CHUNKS, n_ma, 2 * per, LANES), bf16),
            pltpu.VMEM((CHUNKS, n_ma, 2 * per, LANES), bf16),
            pltpu.VMEM((n_ma, 1, LANES), f32),
            pltpu.VMEM((n_ma, 1, LANES), f32),
            pltpu.VMEM((2 * feeds // LANES, LANES), f32),
            pltpu.VMEM((2, cols, LANES), f32),
            pltpu.VMEM((8, rows), f32),
            pltpu.VMEM((n_bl, 2, share_pad), f32),
            pltpu.VMEM((n_bl, 2, share_pad), f32),
            dma((CHUNKS, 2)),
            dma((CHUNKS, 2)),
            dma((3,)),
            dma((CHUNKS, n_ma)),
            dma((CHUNKS, n_ma)),
            dma((n_ma,)),
            dma((n_ma,)),
            dma((n_bl,)),
            dma((n_bl,)),
        ],
        compiler_params=pltpu.CompilerParams(
            collective_id=0, has_side_effects=True, vmem_limit_bytes=56 * 2**20
        ),
        cost_estimate=pl.CostEstimate(
            flops=2 * rows * (2 * local_times * 2 * n_ma + 4 * width),
            bytes_accessed=4 * rows * (local_times + width),
            transcendentals=0,
        ),
    )(visibilities, beam_blocks, feed_pairs.T, feed_gains, m_order)


def solution(mesh):
    return jax.shard_map(
        functools.partial(per_device, mesh.shape["ma"], mesh.shape["bl"]),
        mesh=mesh,
        in_specs=(P(None, "bl", "ma"), P("ma", None, "bl", None), P("bl", None), P(), P()),
        out_specs=P(None, "ma", "bl"),
        check_vma=False,
    )
```

```python
import functools

import jax
import jax.numpy as jnp
import numpy as np
from jax import lax
from jax.experimental import pallas as pl
from jax.experimental.pallas import tpu as pltpu
from jax.sharding import PartitionSpec as P

NT = 8192
LANES = 128
CHUNKS = 2
VMEM_LIMIT = 56 * 2**20
MESH = pl.DeviceIdType.MESH


def trig(k):
    quarter = NT // 4
    turn = (k + quarter // 2) // quarter
    x = (k - turn * quarter).astype(jnp.float32) * np.float32(2.0 * np.pi / NT)
    y = x * x
    sin_x = x * (1.0 + y * (-1.0 / 6 + y * (1.0 / 120 + y * (-1.0 / 5040 + y * (1.0 / 362880)))))
    cos_x = 1.0 + y * (-0.5 + y * (1.0 / 24 + y * (-1.0 / 720 + y * (1.0 / 40320))))
    odd = (turn & 1) == 1
    cos_k = jnp.where(odd, sin_x, cos_x)
    sin_k = jnp.where(odd, cos_x, sin_x)
    cos_k = jnp.where(((turn + 1) & 2) == 2, -cos_k, cos_k)
    sin_k = jnp.where((turn & 2) == 2, -sin_k, sin_k)
    return cos_k, sin_k


def kernel(
    n_ma, n_bl, vis, beam, pairs, gains, order, out,
    vis_v, beam_v, pairs_v, gains_v, order_s,
    sums, near, part, got, rem_sums, rem_near, rem_part, rem_got, table, factor, lhs, share,
    vis_sem, beam_sem, small_sem, near_send, near_recv, send_sem, recv_sem, bl_send, bl_recv,
):
    me = lax.axis_index("ma")
    my_bl = lax.axis_index("bl")
    rows = vis.shape[1]
    local_times = vis.shape[2]
    cols = rows // LANES
    rem = rows - cols * LANES
    per = cols // CHUNKS
    chips = n_ma // 2
    chip = me // 2
    core = lax.rem(me, 2)
    other = 1 - core
    sibling = chip * 2 + other
    far = [lax.rem(chip + k, chips) for k in range(chips)]
    far_order = sorted(range(1, chips), key=lambda k: abs(k - chips // 2))

    barrier = pltpu.get_barrier_semaphore()
    pl.semaphore_signal(barrier, inc=1, device_id={"ma": sibling}, device_id_type=MESH)
    for k in range(1, chips):
        pl.semaphore_signal(barrier, inc=1, device_id={"ma": far[k] * 2 + core}, device_id_type=MESH)
    bl_peers = [lax.rem(my_bl + k, n_bl) for k in range(n_bl)]
    for k in range(1, n_bl):
        pl.semaphore_signal(barrier, inc=1, device_id={"bl": bl_peers[k]}, device_id_type=MESH)

    order_copy = pltpu.make_async_copy(order, order_s, small_sem.at[0])
    order_copy.start()
    spans = [(c * per * LANES, per * LANES) for c in range(CHUNKS)] + [(cols * LANES, rem)]
    load_order = [0, CHUNKS] + list(range(1, CHUNKS))
    vis_copies, beam_copies = {}, {}
    for c in load_order:
        for p in range(2):
            piece = pl.ds(*spans[c])
            vis_copies[c, p] = pltpu.make_async_copy(vis.at[p, piece], vis_v.at[p, piece], vis_sem.at[c, p])
            vis_copies[c, p].start()
            beam_copies[c, p] = pltpu.make_async_copy(beam.at[0, p, piece], beam_v.at[p, piece], beam_sem.at[c, p])
    pairs_copy = pltpu.make_async_copy(pairs, pairs_v, small_sem.at[1])
    pairs_copy.start()
    gains_copy = pltpu.make_async_copy(gains, gains_v, small_sem.at[2])
    gains_copy.start()

    order_copy.wait()
    slot = lax.broadcasted_iota(jnp.int32, (n_ma, LANES), 0)
    m_value = jnp.zeros((n_ma, LANES), jnp.int32)
    for j in range(n_ma):
        m_value = jnp.where(slot == (j % 2) * chips + j // 2, order_s[j] - n_ma // 2, m_value)
    left, right = [], []
    for block in range(local_times // LANES):
        time = me * local_times + block * LANES + lax.broadcasted_iota(jnp.int32, (n_ma, LANES), 1)
        cos_k, sin_k = trig((time * m_value) & (NT - 1))
        scale = np.float32(1.0 / np.sqrt(np.float32(NT)))
        cos_k, sin_k = cos_k * scale, sin_k * scale
        left.append(jnp.concatenate([cos_k, -sin_k], axis=0).astype(jnp.bfloat16))
        right.append(jnp.concatenate([sin_k, cos_k], axis=0).astype(jnp.bfloat16))
    left = jnp.concatenate(left, axis=1)
    right = jnp.concatenate(right, axis=1)

    def transform(start, size):
        contract = (((1,), (1,)), ((), ()))
        re = lax.dot_general(left, vis_v[0, start:start + size, :], contract, preferred_element_type=jnp.float32)
        im = lax.dot_general(right, vis_v[1, start:start + size, :], contract, preferred_element_type=jnp.float32)
        return re + im

    near_copies = {}

    def to_sibling(c, source, target):
        near_copies[c] = pltpu.make_async_remote_copy(
            src_ref=source, dst_ref=target, send_sem=near_send.at[c], recv_sem=near_recv.at[c],
            device_id={"ma": sibling}, device_id_type=MESH,
        )
        near_copies[c].start()

    for c in load_order:
        for p in range(2):
            vis_copies[c, p].wait()
        if c == load_order[-1]:
            for b in load_order:
                for p in range(2):
                    beam_copies[b, p].start()
        if c == CHUNKS:
            flat = transform(*spans[c])
            wide = jnp.concatenate(
                [flat[:n_ma], flat[n_ma:], jnp.zeros((n_ma, LANES - 2 * rem), jnp.float32)], axis=1
            )
            for j in range(n_ma):
                rem_sums[j // chips, j % chips] = wide[j:j + 1, :]
            to_sibling(c, rem_sums.at[other], rem_near)
            continue
        step = 2
        for i in range(0, per, step):
            flat = transform(spans[c][0] + i * LANES, step * LANES)
            for u in range(step):
                for p in range(2):
                    for g in range(2):
                        from_row = p * n_ma + g * chips
                        sums[c, g, pl.ds(p * per + i + u, chips, stride=2 * per), :] = (
                            flat[from_row:from_row + chips, u * LANES:(u + 1) * LANES]
                        )
        if c == 0:
            pl.semaphore_wait(barrier, 1 + chips - 1 + n_bl - 1)
        to_sibling(c, sums.at[c, other], near.at[c])

    far_copies = {}
    for c in load_order:
        near_copies[c].wait_recv()
        if c == CHUNKS:
            rem_part[...] = rem_sums[core] + rem_near[...]
        else:
            both = sums[c, core] + near[c]
            sums[c, core] = both
            part[c] = both.astype(jnp.bfloat16).reshape(chips, 2 * per, LANES)
        for k in far_order:
            source = rem_part.at[far[k]] if c == CHUNKS else part.at[c, far[k]]
            target = rem_got.at[chip] if c == CHUNKS else got.at[c, chip]
            far_copies[c, k] = pltpu.make_async_remote_copy(
                src_ref=source, dst_ref=target, send_sem=send_sem.at[c, k], recv_sem=recv_sem.at[c, k],
                device_id={"ma": far[k] * 2 + core}, device_id_type=MESH,
            )
            far_copies[c, k].start()

    pairs_copy.wait()
    gains_copy.wait()
    high = gains.shape[1] // LANES
    for comp in range(2):
        for h in range(high):
            table[comp * high + h:comp * high + h + 1, :] = gains_v[comp:comp + 1, h * LANES:(h + 1) * LANES]
    whole = table[...]
    first = whole.astype(jnp.bfloat16)
    rest = whole - first.astype(jnp.float32)
    second = rest.astype(jnp.bfloat16)
    third = (rest - second.astype(jnp.float32)).astype(jnp.bfloat16)
    thirds = jnp.concatenate([first, second, third], axis=0)

    def gain_of(feed, start, size):
        index = pairs_v[feed:feed + 1, start:start + size]
        low = lax.broadcasted_iota(jnp.int32, (LANES, size), 0)
        hot = jnp.where(low == (index & (LANES - 1)), 1.0, 0.0).astype(jnp.bfloat16)
        picked = jnp.dot(thirds, hot, preferred_element_type=jnp.float32)
        picked = picked[:2 * high] + picked[2 * high:4 * high] + picked[4 * high:]
        mask = lax.broadcasted_iota(jnp.int32, (high, size), 0) == index // LANES
        re = jnp.sum(jnp.where(mask, picked[:high], 0.0), axis=0, keepdims=True)
        im = jnp.sum(jnp.where(mask, picked[high:], 0.0), axis=0, keepdims=True)
        return re, im

    def factor_of(start, size):
        a_re, a_im = gain_of(0, start, size)
        b_re, b_im = gain_of(1, start, size)
        return a_re * b_re + a_im * b_im, a_im * b_re - a_re * b_im

    for i in range(0, cols, 2):
        f_re, f_im = factor_of(i * LANES, 2 * LANES)
        for u in range(2):
            factor[0, i + u:i + u + 1, :] = f_re[:, u * LANES:(u + 1) * LANES]
            factor[1, i + u:i + u + 1, :] = f_im[:, u * LANES:(u + 1) * LANES]
    rem_re, rem_im = factor_of(*spans[CHUNKS])

    def weigh(s_re, s_im, f_re, f_im):
        s_re = s_re.astype(jnp.bfloat16).astype(jnp.float32)
        s_im = s_im.astype(jnp.bfloat16).astype(jnp.float32)
        return s_re * f_re - s_im * f_im, s_re * f_im + s_im * f_re

    total = None
    for c in load_order:
        for p in range(2):
            beam_copies[c, p].wait()
        for k in far_order:
            far_copies[c, k].wait_recv()
        start, size = spans[c]
        at = slice(start, start + size)
        if c == CHUNKS:
            tail = rem_part[chip]
            for k in far_order:
                tail = tail + rem_got[far[k]]
            w_re, w_im = weigh(tail[:, :rem], tail[:, rem:2 * rem], rem_re, rem_im)
            lhs[0:1, at] = w_re
            lhs[1:2, at] = w_im
        else:
            mine = pl.multiple_of(chip * 2 * per, 2 * per)
            spectra = sums[c, core, pl.ds(mine, 2 * per), :]
            for k in far_order:
                spectra = spectra + got[c, far[k]].astype(jnp.float32)
            w_re, w_im = weigh(
                spectra[:per], spectra[per:], factor[0, c * per:(c + 1) * per], factor[1, c * per:(c + 1) * per]
            )
            for i in range(per):
                lane = slice(start + i * LANES, start + (i + 1) * LANES)
                lhs[0:1, lane] = w_re[i:i + 1]
                lhs[1:2, lane] = w_im[i:i + 1]
        w_re, w_im = lhs[0:1, at], lhs[1:2, at]
        row_a = jnp.concatenate([w_re, w_im], axis=0).astype(jnp.bfloat16)
        row_b = jnp.concatenate([w_im, -w_re], axis=0).astype(jnp.bfloat16)
        term = jnp.dot(row_a, beam_v[0, at, :], preferred_element_type=jnp.float32)
        term = term + jnp.dot(row_b, beam_v[1, at, :], preferred_element_type=jnp.float32)
        total = term if total is None else total + term

    width = beam.shape[3] // n_bl
    for d in range(n_bl):
        share[d, :, 0, 0:width] = total[:, d * width:(d + 1) * width]
    bl_copies = []
    for k in range(1, n_bl):
        copy = pltpu.make_async_remote_copy(
            src_ref=share.at[bl_peers[k]], dst_ref=out.at[my_bl],
            send_sem=bl_send.at[k], recv_sem=bl_recv.at[k],
            device_id={"bl": bl_peers[k]}, device_id_type=MESH,
        )
        copy.start()
        bl_copies.append(copy)
    out[my_bl] = share[my_bl]
    for copy in near_copies.values():
        copy.wait_send()
    for copy in far_copies.values():
        copy.wait_send()
    for copy in bl_copies:
        copy.wait_send()
    for copy in bl_copies:
        copy.wait_recv()


def per_device(n_ma, n_bl, visibilities, beam_blocks, feed_pairs, feed_gains, m_order):
    _, rows, local_times = visibilities.shape
    width = beam_blocks.shape[3]
    assert m_order.shape[0] == n_ma and beam_blocks.shape[0] == 1 and n_ma % 16 == 0
    cols = rows // LANES
    rem = rows - cols * LANES
    per = cols // CHUNKS
    assert cols % (2 * CHUNKS) == 0 and (2 * per) % 16 == 0 and 0 < 2 * rem <= LANES
    chips = n_ma // 2
    share_width = width // n_bl
    share_pad = -(-share_width // LANES) * LANES
    feeds = feed_gains.shape[1]
    f32, bf16 = jnp.float32, jnp.bfloat16
    dma = pltpu.SemaphoreType.DMA
    parts = pl.pallas_call(
        functools.partial(kernel, n_ma, n_bl),
        out_shape=jax.ShapeDtypeStruct((n_bl, 2, 1, share_pad), f32),
        in_specs=[pl.BlockSpec(memory_space=pl.ANY)] * 5,
        out_specs=pl.BlockSpec(memory_space=pltpu.VMEM),
        scratch_shapes=[
            pltpu.VMEM((2, rows, local_times), bf16),
            pltpu.VMEM((2, rows, width), bf16),
            pltpu.VMEM((2, rows), jnp.int32),
            pltpu.VMEM((2, feeds), f32),
            pltpu.SMEM((n_ma,), jnp.int32),
            pltpu.VMEM((CHUNKS, 2, chips * 2 * per, LANES), f32),
            pltpu.VMEM((CHUNKS, chips * 2 * per, LANES), f32),
            pltpu.VMEM((CHUNKS, chips, 2 * per, LANES), bf16),
            pltpu.VMEM((CHUNKS, chips, 2 * per, LANES), bf16),
            pltpu.VMEM((2, chips, 1, LANES), f32),
            pltpu.VMEM((chips, 1, LANES), f32),
            pltpu.VMEM((chips, 1, LANES), f32),
            pltpu.VMEM((chips, 1, LANES), f32),
            pltpu.VMEM((2 * feeds // LANES, LANES), f32),
            pltpu.VMEM((2, cols, LANES), f32),
            pltpu.VMEM((8, rows), f32),
            pltpu.VMEM((n_bl, 2, 1, share_pad), f32),
            dma((CHUNKS + 1, 2)),
            dma((CHUNKS + 1, 2)),
            dma((3,)),
            dma((CHUNKS + 1,)),
            dma((CHUNKS + 1,)),
            dma((CHUNKS + 1, chips)),
            dma((CHUNKS + 1, chips)),
            dma((n_bl,)),
            dma((n_bl,)),
        ],
        compiler_params=pltpu.CompilerParams(
            collective_id=0, has_side_effects=True, vmem_limit_bytes=VMEM_LIMIT
        ),
        cost_estimate=pl.CostEstimate(
            flops=2 * rows * (2 * local_times * 2 * n_ma + 4 * width),
            bytes_accessed=4 * rows * (local_times + width),
            transcendentals=0,
        ),
    )(visibilities, beam_blocks, feed_pairs.T, feed_gains, m_order)
    return jnp.sum(parts[..., :share_width], axis=0)


def solution(mesh):
    return jax.shard_map(
        functools.partial(per_device, mesh.shape["ma"], mesh.shape["bl"]),
        mesh=mesh,
        in_specs=(P(None, "bl", "ma"), P("ma", None, "bl", None), P("bl", None), P(), P()),
        out_specs=P(None, "ma", "bl"),
        check_vma=False,
    )
```

```python
import functools

import jax
import jax.numpy as jnp
import numpy as np
from jax import lax
from jax.experimental import pallas as pl
from jax.experimental.pallas import tpu as pltpu
from jax.sharding import PartitionSpec as P

NT = 8192
LANES = 128
CHUNKS = 2
PIECE = 512
VMEM_LIMIT = 56 * 2**20
MESH = pl.DeviceIdType.MESH


def trig(k):
    quarter = NT // 4
    turn = (k + quarter // 2) // quarter
    x = (k - turn * quarter).astype(jnp.float32) * np.float32(2.0 * np.pi / NT)
    y = x * x
    sin_x = x * (1.0 + y * (-1.0 / 6 + y * (1.0 / 120 + y * (-1.0 / 5040 + y * (1.0 / 362880)))))
    cos_x = 1.0 + y * (-0.5 + y * (1.0 / 24 + y * (-1.0 / 720 + y * (1.0 / 40320))))
    odd = (turn & 1) == 1
    cos_k = jnp.where(odd, sin_x, cos_x)
    sin_k = jnp.where(odd, cos_x, sin_x)
    cos_k = jnp.where(((turn + 1) & 2) == 2, -cos_k, cos_k)
    sin_k = jnp.where((turn & 2) == 2, -sin_k, sin_k)
    return cos_k, sin_k


def kernel(
    n_ma, n_bl, vis, beam, pairs, gains, order, out,
    vis_v, beam_v, pairs_v, gains_v, order_s,
    sums, near, part, got, rem_sums, rem_near, rem_part, rem_got, table, factor, lhs, share,
    vis_sem, beam_sem, small_sem, near_send, near_recv, send_sem, recv_sem, bl_send, bl_recv,
):
    me = lax.axis_index("ma")
    my_bl = lax.axis_index("bl")
    rows = vis.shape[1]
    local_times = vis.shape[2]
    cols = rows // LANES
    rem = rows - cols * LANES
    per = cols // CHUNKS
    chips = n_ma // 2
    chip = me // 2
    core = lax.rem(me, 2)
    other = 1 - core
    sibling = chip * 2 + other
    far = [lax.rem(chip + k, chips) for k in range(chips)]
    far_order = sorted(range(1, chips), key=lambda k: abs(k - chips // 2))

    barrier = pltpu.get_barrier_semaphore()
    pl.semaphore_signal(barrier, inc=1, device_id={"ma": sibling}, device_id_type=MESH)
    for k in range(1, chips):
        pl.semaphore_signal(barrier, inc=1, device_id={"ma": far[k] * 2 + core}, device_id_type=MESH)
    bl_peers = [lax.rem(my_bl + k, n_bl) for k in range(n_bl)]
    for k in range(1, n_bl):
        pl.semaphore_signal(barrier, inc=1, device_id={"bl": bl_peers[k]}, device_id_type=MESH)

    order_copy = pltpu.make_async_copy(order, order_s, small_sem.at[0])
    order_copy.start()
    spans = [(c * per * LANES, per * LANES) for c in range(CHUNKS)] + [(cols * LANES, rem)]
    load_order = [0, CHUNKS] + list(range(1, CHUNKS))
    pieces = {}
    for c in load_order:
        start, size = spans[c]
        pieces[c] = [(at, min(PIECE, start + size - at)) for at in range(start, start + size, PIECE)]
    vis_copies, beam_copies = {}, {}
    slot = 0
    for c in load_order:
        for at, size in pieces[c]:
            for p in range(2):
                piece = pl.ds(at, size)
                vis_copies[at, p] = pltpu.make_async_copy(vis.at[p, piece], vis_v.at[p, piece], vis_sem.at[slot])
                vis_copies[at, p].start()
                beam_copies[at, p] = pltpu.make_async_copy(
                    beam.at[0, p, piece], beam_v.at[p, piece], beam_sem.at[slot]
                )
                slot += 1
    pairs_copy = pltpu.make_async_copy(pairs, pairs_v, small_sem.at[1])
    pairs_copy.start()
    gains_copy = pltpu.make_async_copy(gains, gains_v, small_sem.at[2])
    gains_copy.start()

    order_copy.wait()
    row_of = lax.broadcasted_iota(jnp.int32, (n_ma, LANES), 0)
    m_value = jnp.zeros((n_ma, LANES), jnp.int32)
    for j in range(n_ma):
        m_value = jnp.where(row_of == (j % 2) * chips + j // 2, order_s[j] - n_ma // 2, m_value)
    left, right = [], []
    for block in range(local_times // LANES):
        time = me * local_times + block * LANES + lax.broadcasted_iota(jnp.int32, (n_ma, LANES), 1)
        cos_k, sin_k = trig((time * m_value) & (NT - 1))
        scale = np.float32(1.0 / np.sqrt(np.float32(NT)))
        cos_k, sin_k = cos_k * scale, sin_k * scale
        left.append(jnp.concatenate([cos_k, -sin_k], axis=0).astype(jnp.bfloat16))
        right.append(jnp.concatenate([sin_k, cos_k], axis=0).astype(jnp.bfloat16))
    left = jnp.concatenate(left, axis=1)
    right = jnp.concatenate(right, axis=1)

    def transform(start, size):
        contract = (((1,), (1,)), ((), ()))
        re = lax.dot_general(left, vis_v[0, start:start + size, :], contract, preferred_element_type=jnp.float32)
        im = lax.dot_general(right, vis_v[1, start:start + size, :], contract, preferred_element_type=jnp.float32)
        return re + im

    near_copies = {}

    def to_sibling(c, source, target):
        near_copies[c] = pltpu.make_async_remote_copy(
            src_ref=source, dst_ref=target, send_sem=near_send.at[c], recv_sem=near_recv.at[c],
            device_id={"ma": sibling}, device_id_type=MESH,
        )
        near_copies[c].start()

    far_copies = {}

    def to_far(c):
        near_copies[c].wait_recv()
        if c == CHUNKS:
            rem_part[...] = rem_sums[core] + rem_near[...]
        else:
            both = sums[c, core] + near[c]
            sums[c, core] = both
            part[c] = both.astype(jnp.bfloat16).reshape(chips, 2 * per, LANES)
        for k in far_order:
            source = rem_part.at[far[k]] if c == CHUNKS else part.at[c, far[k]]
            target = rem_got.at[chip] if c == CHUNKS else got.at[c, chip]
            far_copies[c, k] = pltpu.make_async_remote_copy(
                src_ref=source, dst_ref=target, send_sem=send_sem.at[c, k], recv_sem=recv_sem.at[c, k],
                device_id={"ma": far[k] * 2 + core}, device_id_type=MESH,
            )
            far_copies[c, k].start()

    waiting = []
    for c in load_order:
        for number, (at, size) in enumerate(pieces[c]):
            for p in range(2):
                vis_copies[at, p].wait()
            if c == 0 and number == len(pieces[c]) - 1:
                for copy in beam_copies.values():
                    copy.start()
            if c == CHUNKS:
                flat = transform(at, size)
                wide = jnp.concatenate(
                    [flat[:n_ma], flat[n_ma:], jnp.zeros((n_ma, LANES - 2 * rem), jnp.float32)], axis=1
                )
                for j in range(n_ma):
                    rem_sums[j // chips, j % chips] = wide[j:j + 1, :]
                continue
            for begin in range(at, at + size, 2 * LANES):
                flat = transform(begin, 2 * LANES)
                for u in range(2):
                    row = (begin - spans[c][0]) // LANES + u
                    for p in range(2):
                        for g in range(2):
                            from_row = p * n_ma + g * chips
                            sums[c, g, pl.ds(p * per + row, chips, stride=2 * per), :] = (
                                flat[from_row:from_row + chips, u * LANES:(u + 1) * LANES]
                            )
            if number == 0:
                for b in waiting:
                    to_far(b)
                waiting = []
        if c == 0:
            pl.semaphore_wait(barrier, 1 + chips - 1 + n_bl - 1)
        if c == CHUNKS:
            to_sibling(c, rem_sums.at[other], rem_near)
        else:
            to_sibling(c, sums.at[c, other], near.at[c])
        waiting.append(c)

    pairs_copy.wait()
    gains_copy.wait()
    high = gains.shape[1] // LANES
    for comp in range(2):
        for h in range(high):
            table[comp * high + h:comp * high + h + 1, :] = gains_v[comp:comp + 1, h * LANES:(h + 1) * LANES]
    whole = table[...]
    first = whole.astype(jnp.bfloat16)
    rest = whole - first.astype(jnp.float32)
    second = rest.astype(jnp.bfloat16)
    third = (rest - second.astype(jnp.float32)).astype(jnp.bfloat16)
    thirds = jnp.concatenate([first, second, third], axis=0)

    def gain_of(feed, start, size):
        index = pairs_v[feed:feed + 1, start:start + size]
        low = lax.broadcasted_iota(jnp.int32, (LANES, size), 0)
        hot = jnp.where(low == (index & (LANES - 1)), 1.0, 0.0).astype(jnp.bfloat16)
        picked = jnp.dot(thirds, hot, preferred_element_type=jnp.float32)
        picked = picked[:2 * high] + picked[2 * high:4 * high] + picked[4 * high:]
        mask = lax.broadcasted_iota(jnp.int32, (high, size), 0) == index // LANES
        re = jnp.sum(jnp.where(mask, picked[:high], 0.0), axis=0, keepdims=True)
        im = jnp.sum(jnp.where(mask, picked[high:], 0.0), axis=0, keepdims=True)
        return re, im

    def factor_of(start, size):
        a_re, a_im = gain_of(0, start, size)
        b_re, b_im = gain_of(1, start, size)
        return a_re * b_re + a_im * b_im, a_im * b_re - a_re * b_im

    for i in range(0, cols, 2):
        f_re, f_im = factor_of(i * LANES, 2 * LANES)
        for u in range(2):
            factor[0, i + u:i + u + 1, :] = f_re[:, u * LANES:(u + 1) * LANES]
            factor[1, i + u:i + u + 1, :] = f_im[:, u * LANES:(u + 1) * LANES]
    rem_re, rem_im = factor_of(*spans[CHUNKS])

    for b in waiting:
        to_far(b)

    def weigh(s_re, s_im, f_re, f_im):
        s_re = s_re.astype(jnp.bfloat16).astype(jnp.float32)
        s_im = s_im.astype(jnp.bfloat16).astype(jnp.float32)
        return s_re * f_re - s_im * f_im, s_re * f_im + s_im * f_re

    total = None
    for c in load_order:
        for k in far_order:
            far_copies[c, k].wait_recv()
        start, size = spans[c]
        at = slice(start, start + size)
        if c == CHUNKS:
            tail = rem_part[chip]
            for k in far_order:
                tail = tail + rem_got[far[k]]
            w_re, w_im = weigh(tail[:, :rem], tail[:, rem:2 * rem], rem_re, rem_im)
            lhs[0:1, at] = w_re
            lhs[1:2, at] = w_im
        else:
            mine = pl.multiple_of(chip * 2 * per, 2 * per)
            spectra = sums[c, core, pl.ds(mine, 2 * per), :]
            for k in far_order:
                spectra = spectra + got[c, far[k]].astype(jnp.float32)
            w_re, w_im = weigh(
                spectra[:per], spectra[per:], factor[0, c * per:(c + 1) * per], factor[1, c * per:(c + 1) * per]
            )
            for i in range(per):
                lane = slice(start + i * LANES, start + (i + 1) * LANES)
                lhs[0:1, lane] = w_re[i:i + 1]
                lhs[1:2, lane] = w_im[i:i + 1]
        for begin, size in pieces[c]:
            at = slice(begin, begin + size)
            w_re, w_im = lhs[0:1, at], lhs[1:2, at]
            rows_of = [
                jnp.concatenate([w_re, w_im], axis=0).astype(jnp.bfloat16),
                jnp.concatenate([w_im, -w_re], axis=0).astype(jnp.bfloat16),
            ]
            for p in range(2):
                beam_copies[begin, p].wait()
                term = jnp.dot(rows_of[p], beam_v[p, at, :], preferred_element_type=jnp.float32)
                total = term if total is None else total + term

    width = beam.shape[3] // n_bl
    for d in range(n_bl):
        share[d, :, 0, 0:width] = total[:, d * width:(d + 1) * width]
    bl_copies = []
    for k in range(1, n_bl):
        copy = pltpu.make_async_remote_copy(
            src_ref=share.at[bl_peers[k]], dst_ref=out.at[my_bl],
            send_sem=bl_send.at[k], recv_sem=bl_recv.at[k],
            device_id={"bl": bl_peers[k]}, device_id_type=MESH,
        )
        copy.start()
        bl_copies.append(copy)
    out[my_bl] = share[my_bl]
    for copy in near_copies.values():
        copy.wait_send()
    for copy in far_copies.values():
        copy.wait_send()
    for copy in bl_copies:
        copy.wait_send()
    for copy in bl_copies:
        copy.wait_recv()


def per_device(n_ma, n_bl, visibilities, beam_blocks, feed_pairs, feed_gains, m_order):
    _, rows, local_times = visibilities.shape
    width = beam_blocks.shape[3]
    assert m_order.shape[0] == n_ma and beam_blocks.shape[0] == 1 and n_ma % 16 == 0
    cols = rows // LANES
    rem = rows - cols * LANES
    per = cols // CHUNKS
    assert per * LANES % PIECE == 0 and cols % CHUNKS == 0 and (2 * per) % 16 == 0 and 0 < 2 * rem <= LANES
    chips = n_ma // 2
    share_width = width // n_bl
    share_pad = -(-share_width // LANES) * LANES
    feeds = feed_gains.shape[1]
    f32, bf16 = jnp.float32, jnp.bfloat16
    dma = pltpu.SemaphoreType.DMA
    parts = pl.pallas_call(
        functools.partial(kernel, n_ma, n_bl),
        out_shape=jax.ShapeDtypeStruct((n_bl, 2, 1, share_pad), f32),
        in_specs=[pl.BlockSpec(memory_space=pl.ANY)] * 5,
        out_specs=pl.BlockSpec(memory_space=pltpu.VMEM),
        scratch_shapes=[
            pltpu.VMEM((2, rows, local_times), bf16),
            pltpu.VMEM((2, rows, width), bf16),
            pltpu.VMEM((2, rows), jnp.int32),
            pltpu.VMEM((2, feeds), f32),
            pltpu.SMEM((n_ma,), jnp.int32),
            pltpu.VMEM((CHUNKS, 2, chips * 2 * per, LANES), f32),
            pltpu.VMEM((CHUNKS, chips * 2 * per, LANES), f32),
            pltpu.VMEM((CHUNKS, chips, 2 * per, LANES), bf16),
            pltpu.VMEM((CHUNKS, chips, 2 * per, LANES), bf16),
            pltpu.VMEM((2, chips, 1, LANES), f32),
            pltpu.VMEM((chips, 1, LANES), f32),
            pltpu.VMEM((chips, 1, LANES), f32),
            pltpu.VMEM((chips, 1, LANES), f32),
            pltpu.VMEM((2 * feeds // LANES, LANES), f32),
            pltpu.VMEM((2, cols, LANES), f32),
            pltpu.VMEM((8, rows), f32),
            pltpu.VMEM((n_bl, 2, 1, share_pad), f32),
            dma((2 * (cols * LANES // PIECE + 1),)),
            dma((2 * (cols * LANES // PIECE + 1),)),
            dma((3,)),
            dma((CHUNKS + 1,)),
            dma((CHUNKS + 1,)),
            dma((CHUNKS + 1, chips)),
            dma((CHUNKS + 1, chips)),
            dma((n_bl,)),
            dma((n_bl,)),
        ],
        compiler_params=pltpu.CompilerParams(
            collective_id=0, has_side_effects=True, vmem_limit_bytes=VMEM_LIMIT
        ),
        cost_estimate=pl.CostEstimate(
            flops=2 * rows * (2 * local_times * 2 * n_ma + 4 * width),
            bytes_accessed=4 * rows * (local_times + width),
            transcendentals=0,
        ),
    )(visibilities, beam_blocks, feed_pairs.T, feed_gains, m_order)
    result = parts[0, :, :, :share_width]
    for d in range(1, n_bl):
        result = result + parts[d, :, :, :share_width]
    return result


def solution(mesh):
    return jax.shard_map(
        functools.partial(per_device, mesh.shape["ma"], mesh.shape["bl"]),
        mesh=mesh,
        in_specs=(P(None, "bl", "ma"), P("ma", None, "bl", None), P("bl", None), P(), P()),
        out_specs=P(None, "ma", "bl"),
        check_vma=False,
    )
```

```python
import functools

import jax
import jax.numpy as jnp
import numpy as np
from jax import lax
from jax.experimental import pallas as pl
from jax.experimental.pallas import tpu as pltpu
from jax.sharding import PartitionSpec as P

NT = 8192
LANES = 128
CHUNKS = 2
PIECE = 1024
VMEM_LIMIT = 56 * 2**20
MESH = pl.DeviceIdType.MESH


def trig(k):
    quarter = NT // 4
    turn = (k + quarter // 2) // quarter
    x = (k - turn * quarter).astype(jnp.float32) * np.float32(2.0 * np.pi / NT)
    y = x * x
    sin_x = x * (1.0 + y * (-1.0 / 6 + y * (1.0 / 120 + y * (-1.0 / 5040 + y * (1.0 / 362880)))))
    cos_x = 1.0 + y * (-0.5 + y * (1.0 / 24 + y * (-1.0 / 720 + y * (1.0 / 40320))))
    odd = (turn & 1) == 1
    cos_k = jnp.where(odd, sin_x, cos_x)
    sin_k = jnp.where(odd, cos_x, sin_x)
    cos_k = jnp.where(((turn + 1) & 2) == 2, -cos_k, cos_k)
    sin_k = jnp.where((turn & 2) == 2, -sin_k, sin_k)
    return cos_k, sin_k


def kernel(
    n_ma, n_bl, vis, beam, pairs, gains, order, out,
    vis_v, beam_v, pairs_v, gains_v, order_s,
    sums, near, part, got, rem_sums, rem_near, rem_part, rem_got, table, factor, lhs, share,
    vis_sem, beam_sem, small_sem, near_send, near_recv, send_sem, recv_sem, bl_send, bl_recv,
):
    me = lax.axis_index("ma")
    my_bl = lax.axis_index("bl")
    rows = vis.shape[1]
    local_times = vis.shape[2]
    cols = rows // LANES
    rem = rows - cols * LANES
    per = cols // CHUNKS
    chips = n_ma // 2
    chip = me // 2
    core = lax.rem(me, 2)
    other = 1 - core
    sibling = chip * 2 + other
    far = [lax.rem(chip + k, chips) for k in range(chips)]
    far_order = sorted(range(1, chips), key=lambda k: abs(k - chips // 2))

    barrier = pltpu.get_barrier_semaphore()
    pl.semaphore_signal(barrier, inc=1, device_id={"ma": sibling}, device_id_type=MESH)
    for k in range(1, chips):
        pl.semaphore_signal(barrier, inc=1, device_id={"ma": far[k] * 2 + core}, device_id_type=MESH)
    bl_peers = [lax.rem(my_bl + k, n_bl) for k in range(n_bl)]
    for k in range(1, n_bl):
        pl.semaphore_signal(barrier, inc=1, device_id={"bl": bl_peers[k]}, device_id_type=MESH)

    order_copy = pltpu.make_async_copy(order, order_s, small_sem.at[0])
    order_copy.start()
    spans = [(c * per * LANES, per * LANES) for c in range(CHUNKS)] + [(cols * LANES, rem)]
    load_order = [0, CHUNKS] + list(range(1, CHUNKS))
    pieces = {}
    for c in load_order:
        start, size = spans[c]
        pieces[c] = [(at, min(PIECE, start + size - at)) for at in range(start, start + size, PIECE)]
    vis_copies, beam_copies = {}, {}
    slot = 0
    for c in load_order:
        for at, size in pieces[c]:
            for p in range(2):
                piece = pl.ds(at, size)
                vis_copies[at, p] = pltpu.make_async_copy(vis.at[p, piece], vis_v.at[p, piece], vis_sem.at[slot])
                vis_copies[at, p].start()
                beam_copies[at, p] = pltpu.make_async_copy(
                    beam.at[0, p, piece], beam_v.at[p, piece], beam_sem.at[slot]
                )
                slot += 1
    pairs_copy = pltpu.make_async_copy(pairs, pairs_v, small_sem.at[1])
    pairs_copy.start()
    gains_copy = pltpu.make_async_copy(gains, gains_v, small_sem.at[2])
    gains_copy.start()

    order_copy.wait()
    row_of = lax.broadcasted_iota(jnp.int32, (n_ma, LANES), 0)
    m_value = jnp.zeros((n_ma, LANES), jnp.int32)
    for j in range(n_ma):
        m_value = jnp.where(row_of == (j % 2) * chips + j // 2, order_s[j] - n_ma // 2, m_value)
    left, right = [], []
    for block in range(local_times // LANES):
        time = me * local_times + block * LANES + lax.broadcasted_iota(jnp.int32, (n_ma, LANES), 1)
        cos_k, sin_k = trig((time * m_value) & (NT - 1))
        scale = np.float32(1.0 / np.sqrt(np.float32(NT)))
        cos_k, sin_k = cos_k * scale, sin_k * scale
        left.append(jnp.concatenate([cos_k, -sin_k], axis=0).T.astype(jnp.bfloat16))
        right.append(jnp.concatenate([sin_k, cos_k], axis=0).T.astype(jnp.bfloat16))
    left = jnp.concatenate(left, axis=0)
    right = jnp.concatenate(right, axis=0)

    def transform(start, size):
        flat = jnp.dot(vis_v[0, start:start + size, :], left, preferred_element_type=jnp.float32)
        flat = flat + jnp.dot(vis_v[1, start:start + size, :], right, preferred_element_type=jnp.float32)
        return flat.T

    near_copies = {}

    def to_sibling(c, source, target):
        near_copies[c] = pltpu.make_async_remote_copy(
            src_ref=source, dst_ref=target, send_sem=near_send.at[c], recv_sem=near_recv.at[c],
            device_id={"ma": sibling}, device_id_type=MESH,
        )
        near_copies[c].start()

    far_copies = {}

    def to_far(c):
        near_copies[c].wait_recv()
        if c == CHUNKS:
            rem_part[...] = rem_sums[core] + rem_near[...]
        else:
            both = sums[c, core] + near[c]
            sums[c, core] = both
            part[c] = both.astype(jnp.bfloat16).reshape(chips, 2 * per, LANES)
        for k in far_order:
            source = rem_part.at[far[k]] if c == CHUNKS else part.at[c, far[k]]
            target = rem_got.at[chip] if c == CHUNKS else got.at[c, chip]
            far_copies[c, k] = pltpu.make_async_remote_copy(
                src_ref=source, dst_ref=target, send_sem=send_sem.at[c, k], recv_sem=recv_sem.at[c, k],
                device_id={"ma": far[k] * 2 + core}, device_id_type=MESH,
            )
            far_copies[c, k].start()

    for c in load_order:
        for number, (at, size) in enumerate(pieces[c]):
            for p in range(2):
                vis_copies[at, p].wait()
            if c == load_order[-1] and number == 0:
                for copy in beam_copies.values():
                    copy.start()
            if c == CHUNKS:
                flat = transform(at, size)
                wide = jnp.concatenate(
                    [flat[:n_ma], flat[n_ma:], jnp.zeros((n_ma, LANES - 2 * rem), jnp.float32)], axis=1
                )
                for j in range(n_ma):
                    rem_sums[j // chips, j % chips] = wide[j:j + 1, :]
                continue
            for begin in range(at, at + size, 2 * LANES):
                flat = transform(begin, 2 * LANES)
                for u in range(2):
                    row = (begin - spans[c][0]) // LANES + u
                    for p in range(2):
                        for g in range(2):
                            from_row = p * n_ma + g * chips
                            sums[c, g, pl.ds(p * per + row, chips, stride=2 * per), :] = (
                                flat[from_row:from_row + chips, u * LANES:(u + 1) * LANES]
                            )
        if c == 0:
            pl.semaphore_wait(barrier, 1 + chips - 1 + n_bl - 1)
        if c == CHUNKS:
            to_sibling(c, rem_sums.at[other], rem_near)
        else:
            to_sibling(c, sums.at[c, other], near.at[c])

    for c in load_order:
        to_far(c)

    pairs_copy.wait()
    gains_copy.wait()
    high = gains.shape[1] // LANES
    for comp in range(2):
        for h in range(high):
            table[comp * high + h:comp * high + h + 1, :] = gains_v[comp:comp + 1, h * LANES:(h + 1) * LANES]
    whole = table[...]
    first = whole.astype(jnp.bfloat16)
    rest = whole - first.astype(jnp.float32)
    second = rest.astype(jnp.bfloat16)
    third = (rest - second.astype(jnp.float32)).astype(jnp.bfloat16)
    thirds = jnp.concatenate([first, second, third], axis=0)

    def gain_of(feed, start, size):
        index = pairs_v[feed:feed + 1, start:start + size]
        low = lax.broadcasted_iota(jnp.int32, (LANES, size), 0)
        hot = jnp.where(low == (index & (LANES - 1)), 1.0, 0.0).astype(jnp.bfloat16)
        picked = jnp.dot(thirds, hot, preferred_element_type=jnp.float32)
        picked = picked[:2 * high] + picked[2 * high:4 * high] + picked[4 * high:]
        mask = lax.broadcasted_iota(jnp.int32, (high, size), 0) == index // LANES
        re = jnp.sum(jnp.where(mask, picked[:high], 0.0), axis=0, keepdims=True)
        im = jnp.sum(jnp.where(mask, picked[high:], 0.0), axis=0, keepdims=True)
        return re, im

    def factor_of(start, size):
        a_re, a_im = gain_of(0, start, size)
        b_re, b_im = gain_of(1, start, size)
        return a_re * b_re + a_im * b_im, a_im * b_re - a_re * b_im

    for i in range(0, cols, 2):
        f_re, f_im = factor_of(i * LANES, 2 * LANES)
        for u in range(2):
            factor[0, i + u:i + u + 1, :] = f_re[:, u * LANES:(u + 1) * LANES]
            factor[1, i + u:i + u + 1, :] = f_im[:, u * LANES:(u + 1) * LANES]
    rem_re, rem_im = factor_of(*spans[CHUNKS])

    def weigh(s_re, s_im, f_re, f_im):
        s_re = s_re.astype(jnp.bfloat16).astype(jnp.float32)
        s_im = s_im.astype(jnp.bfloat16).astype(jnp.float32)
        return s_re * f_re - s_im * f_im, s_re * f_im + s_im * f_re

    total = None
    for c in load_order:
        for k in far_order:
            far_copies[c, k].wait_recv()
        start, size = spans[c]
        at = slice(start, start + size)
        if c == CHUNKS:
            tail = rem_part[chip]
            for k in far_order:
                tail = tail + rem_got[far[k]]
            w_re, w_im = weigh(tail[:, :rem], tail[:, rem:2 * rem], rem_re, rem_im)
            lhs[0:1, at] = w_re
            lhs[1:2, at] = w_im
        else:
            mine = pl.multiple_of(chip * 2 * per, 2 * per)
            spectra = sums[c, core, pl.ds(mine, 2 * per), :]
            for k in far_order:
                spectra = spectra + got[c, far[k]].astype(jnp.float32)
            w_re, w_im = weigh(
                spectra[:per], spectra[per:], factor[0, c * per:(c + 1) * per], factor[1, c * per:(c + 1) * per]
            )
            for i in range(per):
                lane = slice(start + i * LANES, start + (i + 1) * LANES)
                lhs[0:1, lane] = w_re[i:i + 1]
                lhs[1:2, lane] = w_im[i:i + 1]
        for begin, size in pieces[c]:
            at = slice(begin, begin + size)
            w_re, w_im = lhs[0:1, at], lhs[1:2, at]
            rows_of = [
                jnp.concatenate([w_re, w_im], axis=0).astype(jnp.bfloat16),
                jnp.concatenate([w_im, -w_re], axis=0).astype(jnp.bfloat16),
            ]
            for p in range(2):
                beam_copies[begin, p].wait()
                term = jnp.dot(rows_of[p], beam_v[p, at, :], preferred_element_type=jnp.float32)
                total = term if total is None else total + term

    width = beam.shape[3] // n_bl
    for d in range(n_bl):
        share[d, :, 0, 0:width] = total[:, d * width:(d + 1) * width]
    bl_copies = []
    for k in range(1, n_bl):
        copy = pltpu.make_async_remote_copy(
            src_ref=share.at[bl_peers[k]], dst_ref=out.at[my_bl],
            send_sem=bl_send.at[k], recv_sem=bl_recv.at[k],
            device_id={"bl": bl_peers[k]}, device_id_type=MESH,
        )
        copy.start()
        bl_copies.append(copy)
    out[my_bl] = share[my_bl]
    for copy in near_copies.values():
        copy.wait_send()
    for copy in far_copies.values():
        copy.wait_send()
    for copy in bl_copies:
        copy.wait_send()
    for copy in bl_copies:
        copy.wait_recv()


def per_device(n_ma, n_bl, visibilities, beam_blocks, feed_pairs, feed_gains, m_order):
    _, rows, local_times = visibilities.shape
    width = beam_blocks.shape[3]
    assert m_order.shape[0] == n_ma and beam_blocks.shape[0] == 1 and n_ma % 16 == 0
    cols = rows // LANES
    rem = rows - cols * LANES
    per = cols // CHUNKS
    assert per * LANES % PIECE == 0 and cols % CHUNKS == 0 and (2 * per) % 16 == 0 and 0 < 2 * rem <= LANES
    chips = n_ma // 2
    share_width = width // n_bl
    share_pad = -(-share_width // LANES) * LANES
    feeds = feed_gains.shape[1]
    f32, bf16 = jnp.float32, jnp.bfloat16
    dma = pltpu.SemaphoreType.DMA
    parts = pl.pallas_call(
        functools.partial(kernel, n_ma, n_bl),
        out_shape=jax.ShapeDtypeStruct((n_bl, 2, 1, share_pad), f32),
        in_specs=[pl.BlockSpec(memory_space=pl.ANY)] * 5,
        out_specs=pl.BlockSpec(memory_space=pltpu.VMEM),
        scratch_shapes=[
            pltpu.VMEM((2, rows, local_times), bf16),
            pltpu.VMEM((2, rows, width), bf16),
            pltpu.VMEM((2, rows), jnp.int32),
            pltpu.VMEM((2, feeds), f32),
            pltpu.SMEM((n_ma,), jnp.int32),
            pltpu.VMEM((CHUNKS, 2, chips * 2 * per, LANES), f32),
            pltpu.VMEM((CHUNKS, chips * 2 * per, LANES), f32),
            pltpu.VMEM((CHUNKS, chips, 2 * per, LANES), bf16),
            pltpu.VMEM((CHUNKS, chips, 2 * per, LANES), bf16),
            pltpu.VMEM((2, chips, 1, LANES), f32),
            pltpu.VMEM((chips, 1, LANES), f32),
            pltpu.VMEM((chips, 1, LANES), f32),
            pltpu.VMEM((chips, 1, LANES), f32),
            pltpu.VMEM((2 * feeds // LANES, LANES), f32),
            pltpu.VMEM((2, cols, LANES), f32),
            pltpu.VMEM((8, rows), f32),
            pltpu.VMEM((n_bl, 2, 1, share_pad), f32),
            dma((2 * (cols * LANES // PIECE + 1),)),
            dma((2 * (cols * LANES // PIECE + 1),)),
            dma((3,)),
            dma((CHUNKS + 1,)),
            dma((CHUNKS + 1,)),
            dma((CHUNKS + 1, chips)),
            dma((CHUNKS + 1, chips)),
            dma((n_bl,)),
            dma((n_bl,)),
        ],
        compiler_params=pltpu.CompilerParams(
            collective_id=0, has_side_effects=True, vmem_limit_bytes=VMEM_LIMIT
        ),
        cost_estimate=pl.CostEstimate(
            flops=2 * rows * (2 * local_times * 2 * n_ma + 4 * width),
            bytes_accessed=4 * rows * (local_times + width),
            transcendentals=0,
        ),
    )(visibilities, beam_blocks, feed_pairs.T, feed_gains, m_order)
    result = parts[0, :, :, :share_width]
    for d in range(1, n_bl):
        result = result + parts[d, :, :, :share_width]
    return result


def solution(mesh):
    return jax.shard_map(
        functools.partial(per_device, mesh.shape["ma"], mesh.shape["bl"]),
        mesh=mesh,
        in_specs=(P(None, "bl", "ma"), P("ma", None, "bl", None), P("bl", None), P(), P()),
        out_specs=P(None, "ma", "bl"),
        check_vma=False,
    )
```

```python
import functools

import jax
import jax.numpy as jnp
import numpy as np
from jax import lax
from jax.experimental import pallas as pl
from jax.experimental.pallas import tpu as pltpu
from jax.sharding import PartitionSpec as P

NT = 8192
LANES = 128
CHUNKS = 2
PIECE = 1024
VMEM_LIMIT = 52 * 2**20
MESH = pl.DeviceIdType.MESH


def trig(k):
    quarter = NT // 4
    turn = (k + quarter // 2) // quarter
    x = (k - turn * quarter).astype(jnp.float32) * np.float32(2.0 * np.pi / NT)
    y = x * x
    sin_x = x * (1.0 + y * (-1.0 / 6 + y * (1.0 / 120 + y * (-1.0 / 5040 + y * (1.0 / 362880)))))
    cos_x = 1.0 + y * (-0.5 + y * (1.0 / 24 + y * (-1.0 / 720 + y * (1.0 / 40320))))
    odd = (turn & 1) == 1
    cos_k = jnp.where(odd, sin_x, cos_x)
    sin_k = jnp.where(odd, cos_x, sin_x)
    cos_k = jnp.where(((turn + 1) & 2) == 2, -cos_k, cos_k)
    sin_k = jnp.where((turn & 2) == 2, -sin_k, sin_k)
    return cos_k, sin_k


def kernel(
    n_ma, n_bl, vis, beam, pairs, gains, order, out,
    vis_v, beam_v, pairs_v, gains_v, order_s,
    sums, near, part, got, rem_sums, rem_near, rem_part, rem_got, table, factor, lhs, share,
    vis_sem, beam_sem, small_sem, near_send, near_recv, send_sem, recv_sem, bl_send, bl_recv,
):
    me = lax.axis_index("ma")
    my_bl = lax.axis_index("bl")
    rows = vis.shape[1]
    local_times = vis.shape[2]
    cols = rows // LANES
    rem = rows - cols * LANES
    per = cols // CHUNKS
    chips = n_ma // 2
    chip = me // 2
    core = lax.rem(me, 2)
    other = 1 - core
    sibling = chip * 2 + other
    far = [lax.rem(chip + k, chips) for k in range(chips)]
    far_order = sorted(range(1, chips), key=lambda k: abs(k - chips // 2))

    barrier = pltpu.get_barrier_semaphore()
    pl.semaphore_signal(barrier, inc=1, device_id={"ma": sibling}, device_id_type=MESH)
    for k in range(1, chips):
        pl.semaphore_signal(barrier, inc=1, device_id={"ma": far[k] * 2 + core}, device_id_type=MESH)
    bl_peers = [lax.rem(my_bl + k, n_bl) for k in range(n_bl)]
    for k in range(1, n_bl):
        pl.semaphore_signal(barrier, inc=1, device_id={"bl": bl_peers[k]}, device_id_type=MESH)

    order_copy = pltpu.make_async_copy(order, order_s, small_sem.at[0])
    order_copy.start()
    spans = [(c * per * LANES, per * LANES) for c in range(CHUNKS)] + [(cols * LANES, rem)]
    load_order = [0, CHUNKS] + list(range(1, CHUNKS))
    pieces = {}
    for c in load_order:
        start, size = spans[c]
        pieces[c] = [(at, min(PIECE, start + size - at)) for at in range(start, start + size, PIECE)]
    vis_copies, beam_copies = {}, {}
    slot = 0
    for c in load_order:
        for at, size in pieces[c]:
            for p in range(2):
                piece = pl.ds(at, size)
                vis_copies[at, p] = pltpu.make_async_copy(vis.at[p, piece], vis_v.at[p, piece], vis_sem.at[slot])
                vis_copies[at, p].start()
                beam_copies[at, p] = pltpu.make_async_copy(
                    beam.at[0, p, piece], beam_v.at[p, piece], beam_sem.at[slot]
                )
                slot += 1
    pairs_copy = pltpu.make_async_copy(pairs, pairs_v, small_sem.at[1])
    pairs_copy.start()
    gains_copy = pltpu.make_async_copy(gains, gains_v, small_sem.at[2])
    gains_copy.start()

    order_copy.wait()
    row_of = lax.broadcasted_iota(jnp.int32, (n_ma, LANES), 0)
    m_value = jnp.zeros((n_ma, LANES), jnp.int32)
    for j in range(n_ma):
        m_value = jnp.where(row_of == (j % 2) * chips + j // 2, order_s[j] - n_ma // 2, m_value)
    left, right = [], []
    for block in range(local_times // LANES):
        time = me * local_times + block * LANES + lax.broadcasted_iota(jnp.int32, (n_ma, LANES), 1)
        cos_k, sin_k = trig((time * m_value) & (NT - 1))
        scale = np.float32(1.0 / np.sqrt(np.float32(NT)))
        cos_k, sin_k = cos_k * scale, sin_k * scale
        left.append(jnp.concatenate([cos_k, -sin_k], axis=0).T.astype(jnp.bfloat16))
        right.append(jnp.concatenate([sin_k, cos_k], axis=0).T.astype(jnp.bfloat16))
    left = jnp.concatenate(left, axis=0)
    right = jnp.concatenate(right, axis=0)

    def transform(start, size):
        flat = jnp.dot(vis_v[0, start:start + size, :], left, preferred_element_type=jnp.float32)
        flat = flat + jnp.dot(vis_v[1, start:start + size, :], right, preferred_element_type=jnp.float32)
        return flat.T

    near_copies = {}

    def to_sibling(c, source, target):
        near_copies[c] = pltpu.make_async_remote_copy(
            src_ref=source, dst_ref=target, send_sem=near_send.at[c], recv_sem=near_recv.at[c],
            device_id={"ma": sibling}, device_id_type=MESH,
        )
        near_copies[c].start()

    def start_beam(which):
        for c in which:
            for at, _ in pieces[c]:
                for p in range(2):
                    beam_copies[at, p].start()

    far_copies = {}

    def to_far(c):
        near_copies[c].wait_recv()
        if c == CHUNKS:
            rem_part[...] = rem_sums[core] + rem_near[...]
        else:
            both = sums[c, core] + near[c]
            sums[c, core] = both
            part[c] = both.astype(jnp.bfloat16).reshape(chips, 2 * per, LANES)
        for k in far_order:
            source = rem_part.at[far[k]] if c == CHUNKS else part.at[c, far[k]]
            target = rem_got.at[chip] if c == CHUNKS else got.at[c, chip]
            far_copies[c, k] = pltpu.make_async_remote_copy(
                src_ref=source, dst_ref=target, send_sem=send_sem.at[c, k], recv_sem=recv_sem.at[c, k],
                device_id={"ma": far[k] * 2 + core}, device_id_type=MESH,
            )
            far_copies[c, k].start()

    for c in load_order:
        for number, (at, size) in enumerate(pieces[c]):
            for p in range(2):
                vis_copies[at, p].wait()
            if c == load_order[-1] and number == 0:
                start_beam(load_order[:-1])
            if c == CHUNKS:
                flat = transform(at, size)
                wide = jnp.concatenate(
                    [flat[:n_ma], flat[n_ma:], jnp.zeros((n_ma, LANES - 2 * rem), jnp.float32)], axis=1
                )
                for j in range(n_ma):
                    rem_sums[j // chips, j % chips] = wide[j:j + 1, :]
                continue
            for begin in range(at, at + size, 2 * LANES):
                flat = transform(begin, 2 * LANES)
                for u in range(2):
                    row = (begin - spans[c][0]) // LANES + u
                    for p in range(2):
                        for g in range(2):
                            from_row = p * n_ma + g * chips
                            sums[c, g, pl.ds(p * per + row, chips, stride=2 * per), :] = (
                                flat[from_row:from_row + chips, u * LANES:(u + 1) * LANES]
                            )
        if c == 0:
            pl.semaphore_wait(barrier, 1 + chips - 1 + n_bl - 1)
        if c == CHUNKS:
            to_sibling(c, rem_sums.at[other], rem_near)
        else:
            to_sibling(c, sums.at[c, other], near.at[c])

    for c in load_order:
        if c == load_order[-1]:
            start_beam([c])
        to_far(c)

    pairs_copy.wait()
    gains_copy.wait()
    high = gains.shape[1] // LANES
    for comp in range(2):
        for h in range(high):
            table[comp * high + h:comp * high + h + 1, :] = gains_v[comp:comp + 1, h * LANES:(h + 1) * LANES]
    whole = table[...]
    first = whole.astype(jnp.bfloat16)
    rest = whole - first.astype(jnp.float32)
    second = rest.astype(jnp.bfloat16)
    third = (rest - second.astype(jnp.float32)).astype(jnp.bfloat16)
    thirds = jnp.concatenate([first, second, third], axis=0)

    def gain_of(feed, start, size):
        index = pairs_v[feed:feed + 1, start:start + size]
        low = lax.broadcasted_iota(jnp.int32, (LANES, size), 0)
        hot = jnp.where(low == (index & (LANES - 1)), 1.0, 0.0).astype(jnp.bfloat16)
        picked = jnp.dot(thirds, hot, preferred_element_type=jnp.float32)
        picked = picked[:2 * high] + picked[2 * high:4 * high] + picked[4 * high:]
        mask = lax.broadcasted_iota(jnp.int32, (high, size), 0) == index // LANES
        re = jnp.sum(jnp.where(mask, picked[:high], 0.0), axis=0, keepdims=True)
        im = jnp.sum(jnp.where(mask, picked[high:], 0.0), axis=0, keepdims=True)
        return re, im

    def factor_of(start, size):
        a_re, a_im = gain_of(0, start, size)
        b_re, b_im = gain_of(1, start, size)
        return a_re * b_re + a_im * b_im, a_im * b_re - a_re * b_im

    for i in range(0, cols, 2):
        f_re, f_im = factor_of(i * LANES, 2 * LANES)
        for u in range(2):
            factor[0, i + u:i + u + 1, :] = f_re[:, u * LANES:(u + 1) * LANES]
            factor[1, i + u:i + u + 1, :] = f_im[:, u * LANES:(u + 1) * LANES]
    rem_re, rem_im = factor_of(*spans[CHUNKS])

    def weigh(s_re, s_im, f_re, f_im):
        s_re = s_re.astype(jnp.bfloat16).astype(jnp.float32)
        s_im = s_im.astype(jnp.bfloat16).astype(jnp.float32)
        return s_re * f_re - s_im * f_im, s_re * f_im + s_im * f_re

    total = None
    for c in load_order:
        for k in far_order:
            far_copies[c, k].wait_recv()
        start, size = spans[c]
        at = slice(start, start + size)
        if c == CHUNKS:
            tail = rem_part[chip]
            for k in far_order:
                tail = tail + rem_got[far[k]]
            w_re, w_im = weigh(tail[:, :rem], tail[:, rem:2 * rem], rem_re, rem_im)
            lhs[0:1, at] = w_re
            lhs[1:2, at] = w_im
        else:
            mine = pl.multiple_of(chip * 2 * per, 2 * per)
            spectra = sums[c, core, pl.ds(mine, 2 * per), :]
            for k in far_order:
                spectra = spectra + got[c, far[k]].astype(jnp.float32)
            w_re, w_im = weigh(
                spectra[:per], spectra[per:], factor[0, c * per:(c + 1) * per], factor[1, c * per:(c + 1) * per]
            )
            for i in range(per):
                lane = slice(start + i * LANES, start + (i + 1) * LANES)
                lhs[0:1, lane] = w_re[i:i + 1]
                lhs[1:2, lane] = w_im[i:i + 1]
        for begin, size in pieces[c]:
            at = slice(begin, begin + size)
            w_re, w_im = lhs[0:1, at], lhs[1:2, at]
            rows_of = [
                jnp.concatenate([w_re, w_im], axis=0).astype(jnp.bfloat16),
                jnp.concatenate([w_im, -w_re], axis=0).astype(jnp.bfloat16),
            ]
            for p in range(2):
                beam_copies[begin, p].wait()
                term = jnp.dot(rows_of[p], beam_v[p, at, :], preferred_element_type=jnp.float32)
                total = term if total is None else total + term

    width = beam.shape[3] // n_bl
    for d in range(n_bl):
        share[d, :, 0, 0:width] = total[:, d * width:(d + 1) * width]
    bl_copies = []
    for k in range(1, n_bl):
        copy = pltpu.make_async_remote_copy(
            src_ref=share.at[bl_peers[k]], dst_ref=out.at[my_bl],
            send_sem=bl_send.at[k], recv_sem=bl_recv.at[k],
            device_id={"bl": bl_peers[k]}, device_id_type=MESH,
        )
        copy.start()
        bl_copies.append(copy)
    out[my_bl] = share[my_bl]
    for copy in near_copies.values():
        copy.wait_send()
    for copy in far_copies.values():
        copy.wait_send()
    for copy in bl_copies:
        copy.wait_send()
    for copy in bl_copies:
        copy.wait_recv()


def per_device(n_ma, n_bl, visibilities, beam_blocks, feed_pairs, feed_gains, m_order):
    _, rows, local_times = visibilities.shape
    width = beam_blocks.shape[3]
    assert m_order.shape[0] == n_ma and beam_blocks.shape[0] == 1 and n_ma % 16 == 0
    cols = rows // LANES
    rem = rows - cols * LANES
    per = cols // CHUNKS
    assert per * LANES % PIECE == 0 and cols % CHUNKS == 0 and (2 * per) % 16 == 0 and 0 < 2 * rem <= LANES
    chips = n_ma // 2
    share_width = width // n_bl
    share_pad = -(-share_width // LANES) * LANES
    feeds = feed_gains.shape[1]
    f32, bf16 = jnp.float32, jnp.bfloat16
    dma = pltpu.SemaphoreType.DMA
    parts = pl.pallas_call(
        functools.partial(kernel, n_ma, n_bl),
        out_shape=jax.ShapeDtypeStruct((n_bl, 2, 1, share_pad), f32),
        in_specs=[pl.BlockSpec(memory_space=pl.ANY)] * 5,
        out_specs=pl.BlockSpec(memory_space=pltpu.VMEM),
        scratch_shapes=[
            pltpu.VMEM((2, rows, local_times), bf16),
            pltpu.VMEM((2, rows, width), bf16),
            pltpu.VMEM((2, rows), jnp.int32),
            pltpu.VMEM((2, feeds), f32),
            pltpu.SMEM((n_ma,), jnp.int32),
            pltpu.VMEM((CHUNKS, 2, chips * 2 * per, LANES), f32),
            pltpu.VMEM((CHUNKS, chips * 2 * per, LANES), f32),
            pltpu.VMEM((CHUNKS, chips, 2 * per, LANES), bf16),
            pltpu.VMEM((CHUNKS, chips, 2 * per, LANES), bf16),
            pltpu.VMEM((2, chips, 1, LANES), f32),
            pltpu.VMEM((chips, 1, LANES), f32),
            pltpu.VMEM((chips, 1, LANES), f32),
            pltpu.VMEM((chips, 1, LANES), f32),
            pltpu.VMEM((2 * feeds // LANES, LANES), f32),
            pltpu.VMEM((2, cols, LANES), f32),
            pltpu.VMEM((8, rows), f32),
            pltpu.VMEM((n_bl, 2, 1, share_pad), f32),
            dma((2 * (cols * LANES // PIECE + 1),)),
            dma((2 * (cols * LANES // PIECE + 1),)),
            dma((3,)),
            dma((CHUNKS + 1,)),
            dma((CHUNKS + 1,)),
            dma((CHUNKS + 1, chips)),
            dma((CHUNKS + 1, chips)),
            dma((n_bl,)),
            dma((n_bl,)),
        ],
        compiler_params=pltpu.CompilerParams(
            collective_id=0, has_side_effects=True, vmem_limit_bytes=VMEM_LIMIT
        ),
        cost_estimate=pl.CostEstimate(
            flops=2 * rows * (2 * local_times * 2 * n_ma + 4 * width),
            bytes_accessed=4 * rows * (local_times + width),
            transcendentals=0,
        ),
    )(visibilities, beam_blocks, feed_pairs.T, feed_gains, m_order)
    result = parts[0, :, :, :share_width]
    for d in range(1, n_bl):
        result = result + parts[d, :, :, :share_width]
    return result


def solution(mesh):
    return jax.shard_map(
        functools.partial(per_device, mesh.shape["ma"], mesh.shape["bl"]),
        mesh=mesh,
        in_specs=(P(None, "bl", "ma"), P("ma", None, "bl", None), P("bl", None), P(), P()),
        out_specs=P(None, "ma", "bl"),
        check_vma=False,
    )
```

```python
import functools

import jax
import jax.numpy as jnp
import numpy as np
from jax import lax
from jax.experimental import pallas as pl
from jax.experimental.pallas import tpu as pltpu
from jax.sharding import PartitionSpec as P

NT = 8192
LANES = 128
CHUNKS = 2
PIECE = 1024
VMEM_LIMIT = 55216 * 2**10
MESH = pl.DeviceIdType.MESH


def trig(k):
    quarter = NT // 4
    turn = (k + quarter // 2) // quarter
    x = (k - turn * quarter).astype(jnp.float32) * np.float32(2.0 * np.pi / NT)
    y = x * x
    sin_x = x * (1.0 + y * (-1.0 / 6 + y * (1.0 / 120 + y * (-1.0 / 5040 + y * (1.0 / 362880)))))
    cos_x = 1.0 + y * (-0.5 + y * (1.0 / 24 + y * (-1.0 / 720 + y * (1.0 / 40320))))
    odd = (turn & 1) == 1
    cos_k = jnp.where(odd, sin_x, cos_x)
    sin_k = jnp.where(odd, cos_x, sin_x)
    cos_k = jnp.where(((turn + 1) & 2) == 2, -cos_k, cos_k)
    sin_k = jnp.where((turn & 2) == 2, -sin_k, sin_k)
    return cos_k, sin_k


def kernel(
    n_ma, n_bl, vis, beam, pairs, gains, order, out,
    vis_v, beam_v, pairs_v, gains_v, order_s,
    sums, near, part, got, rem_sums, rem_near, rem_part, rem_got, table, factor, lhs, share,
    vis_sem, beam_sem, small_sem, near_send, near_recv, send_sem, recv_sem, bl_send, bl_recv,
):
    me = lax.axis_index("ma")
    my_bl = lax.axis_index("bl")
    rows = vis.shape[1]
    local_times = vis.shape[2]
    cols = rows // LANES
    rem = rows - cols * LANES
    per = cols // CHUNKS
    chips = n_ma // 2
    chip = me // 2
    core = lax.rem(me, 2)
    other = 1 - core
    sibling = chip * 2 + other
    far = [lax.rem(chip + k, chips) for k in range(chips)]
    far_order = sorted(range(1, chips), key=lambda k: abs(k - chips // 2))

    order_copy = pltpu.make_async_copy(order, order_s, small_sem.at[0])
    order_copy.start()
    spans = [(c * per * LANES, per * LANES) for c in range(CHUNKS)] + [(cols * LANES, rem)]
    load_order = [0, CHUNKS] + list(range(1, CHUNKS))
    pieces = {}
    for c in load_order:
        start, size = spans[c]
        pieces[c] = [(at, min(PIECE, start + size - at)) for at in range(start, start + size, PIECE)]
    vis_copies, beam_copies = {}, {}
    slot = 0
    for c in load_order:
        for at, size in pieces[c]:
            for p in range(2):
                piece = pl.ds(at, size)
                vis_copies[at, p] = pltpu.make_async_copy(vis.at[p, piece], vis_v.at[p, piece], vis_sem.at[slot])
                vis_copies[at, p].start()
                beam_copies[at, p] = pltpu.make_async_copy(
                    beam.at[0, p, piece], beam_v.at[p, piece], beam_sem.at[slot]
                )
                slot += 1
    pairs_copy = pltpu.make_async_copy(pairs, pairs_v, small_sem.at[1])
    pairs_copy.start()
    gains_copy = pltpu.make_async_copy(gains, gains_v, small_sem.at[2])
    gains_copy.start()

    barrier = pltpu.get_barrier_semaphore()
    pl.semaphore_signal(barrier, inc=1, device_id={"ma": sibling}, device_id_type=MESH)
    for k in range(1, chips):
        pl.semaphore_signal(barrier, inc=1, device_id={"ma": far[k] * 2 + core}, device_id_type=MESH)
    bl_peers = [lax.rem(my_bl + k, n_bl) for k in range(n_bl)]
    for k in range(1, n_bl):
        pl.semaphore_signal(barrier, inc=1, device_id={"bl": bl_peers[k]}, device_id_type=MESH)

    order_copy.wait()
    row_of = lax.broadcasted_iota(jnp.int32, (n_ma, LANES), 0)
    m_value = jnp.zeros((n_ma, LANES), jnp.int32)
    for j in range(n_ma):
        m_value = jnp.where(row_of == (j % 2) * chips + j // 2, order_s[j] - n_ma // 2, m_value)
    left, right = [], []
    for block in range(local_times // LANES):
        time = me * local_times + block * LANES + lax.broadcasted_iota(jnp.int32, (n_ma, LANES), 1)
        cos_k, sin_k = trig((time * m_value) & (NT - 1))
        scale = np.float32(1.0 / np.sqrt(np.float32(NT)))
        cos_k, sin_k = cos_k * scale, sin_k * scale
        left.append(jnp.concatenate([cos_k, -sin_k], axis=0).T.astype(jnp.bfloat16))
        right.append(jnp.concatenate([sin_k, cos_k], axis=0).T.astype(jnp.bfloat16))
    left = jnp.concatenate(left, axis=0)
    right = jnp.concatenate(right, axis=0)

    def transform(start, size):
        flat = jnp.dot(vis_v[0, start:start + size, :], left, preferred_element_type=jnp.float32)
        flat = flat + jnp.dot(vis_v[1, start:start + size, :], right, preferred_element_type=jnp.float32)
        return flat.T

    near_copies = {}

    def to_sibling(c, source, target):
        near_copies[c] = pltpu.make_async_remote_copy(
            src_ref=source, dst_ref=target, send_sem=near_send.at[c], recv_sem=near_recv.at[c],
            device_id={"ma": sibling}, device_id_type=MESH,
        )
        near_copies[c].start()

    def start_beam(which):
        for c in which:
            for at, _ in pieces[c]:
                for p in range(2):
                    beam_copies[at, p].start()

    far_copies = {}

    def to_far(c):
        near_copies[c].wait_recv()
        if c == CHUNKS:
            rem_part[...] = rem_sums[core] + rem_near[...]
        else:
            both = sums[c, core] + near[c]
            sums[c, core] = both
            part[c] = both.astype(jnp.bfloat16).reshape(chips, 2 * per, LANES)
        for k in far_order:
            source = rem_part.at[far[k]] if c == CHUNKS else part.at[c, far[k]]
            target = rem_got.at[chip] if c == CHUNKS else got.at[c, chip]
            far_copies[c, k] = pltpu.make_async_remote_copy(
                src_ref=source, dst_ref=target, send_sem=send_sem.at[c, k], recv_sem=recv_sem.at[c, k],
                device_id={"ma": far[k] * 2 + core}, device_id_type=MESH,
            )
            far_copies[c, k].start()

    for c in load_order:
        for number, (at, size) in enumerate(pieces[c]):
            for p in range(2):
                vis_copies[at, p].wait()
            if c == load_order[-1] and number == 0:
                start_beam(load_order[:-1])
            if c == CHUNKS:
                flat = transform(at, size)
                wide = jnp.concatenate(
                    [flat[:n_ma], flat[n_ma:], jnp.zeros((n_ma, LANES - 2 * rem), jnp.float32)], axis=1
                )
                for j in range(n_ma):
                    rem_sums[j // chips, j % chips] = wide[j:j + 1, :]
                continue
            for begin in range(at, at + size, 2 * LANES):
                flat = transform(begin, 2 * LANES)
                for u in range(2):
                    row = (begin - spans[c][0]) // LANES + u
                    for p in range(2):
                        for g in range(2):
                            from_row = p * n_ma + g * chips
                            sums[c, g, pl.ds(p * per + row, chips, stride=2 * per), :] = (
                                flat[from_row:from_row + chips, u * LANES:(u + 1) * LANES]
                            )
        if c == 0:
            pl.semaphore_wait(barrier, 1 + chips - 1 + n_bl - 1)
        if c == CHUNKS:
            to_sibling(c, rem_sums.at[other], rem_near)
        else:
            to_sibling(c, sums.at[c, other], near.at[c])

    for c in load_order[:-1]:
        to_far(c)
    start_beam(load_order[-1:])

    pairs_copy.wait()
    gains_copy.wait()
    high = gains.shape[1] // LANES
    for comp in range(2):
        for h in range(high):
            table[comp * high + h:comp * high + h + 1, :] = gains_v[comp:comp + 1, h * LANES:(h + 1) * LANES]
    whole = table[...]
    first = whole.astype(jnp.bfloat16)
    rest = whole - first.astype(jnp.float32)
    second = rest.astype(jnp.bfloat16)
    third = (rest - second.astype(jnp.float32)).astype(jnp.bfloat16)
    thirds = jnp.concatenate([first, second, third], axis=0)

    def gain_of(feed, start, size):
        index = pairs_v[feed:feed + 1, start:start + size]
        low = lax.broadcasted_iota(jnp.int32, (LANES, size), 0)
        hot = jnp.where(low == (index & (LANES - 1)), 1.0, 0.0).astype(jnp.bfloat16)
        picked = jnp.dot(thirds, hot, preferred_element_type=jnp.float32)
        picked = picked[:2 * high] + picked[2 * high:4 * high] + picked[4 * high:]
        mask = lax.broadcasted_iota(jnp.int32, (high, size), 0) == index // LANES
        re = jnp.sum(jnp.where(mask, picked[:high], 0.0), axis=0, keepdims=True)
        im = jnp.sum(jnp.where(mask, picked[high:], 0.0), axis=0, keepdims=True)
        return re, im

    def factor_of(start, size):
        a_re, a_im = gain_of(0, start, size)
        b_re, b_im = gain_of(1, start, size)
        return a_re * b_re + a_im * b_im, a_im * b_re - a_re * b_im

    for i in range(0, cols, 2):
        f_re, f_im = factor_of(i * LANES, 2 * LANES)
        for u in range(2):
            factor[0, i + u:i + u + 1, :] = f_re[:, u * LANES:(u + 1) * LANES]
            factor[1, i + u:i + u + 1, :] = f_im[:, u * LANES:(u + 1) * LANES]
    rem_re, rem_im = factor_of(*spans[CHUNKS])

    to_far(load_order[-1])

    def weigh(s_re, s_im, f_re, f_im):
        s_re = s_re.astype(jnp.bfloat16).astype(jnp.float32)
        s_im = s_im.astype(jnp.bfloat16).astype(jnp.float32)
        return s_re * f_re - s_im * f_im, s_re * f_im + s_im * f_re

    total = None
    for c in load_order:
        for k in far_order:
            far_copies[c, k].wait_recv()
        start, size = spans[c]
        at = slice(start, start + size)
        if c == CHUNKS:
            tail = rem_part[chip]
            for k in far_order:
                tail = tail + rem_got[far[k]]
            w_re, w_im = weigh(tail[:, :rem], tail[:, rem:2 * rem], rem_re, rem_im)
            lhs[0:1, at] = w_re
            lhs[1:2, at] = w_im
        else:
            mine = pl.multiple_of(chip * 2 * per, 2 * per)
            spectra = sums[c, core, pl.ds(mine, 2 * per), :]
            for k in far_order:
                spectra = spectra + got[c, far[k]].astype(jnp.float32)
            w_re, w_im = weigh(
                spectra[:per], spectra[per:], factor[0, c * per:(c + 1) * per], factor[1, c * per:(c + 1) * per]
            )
            for i in range(per):
                lane = slice(start + i * LANES, start + (i + 1) * LANES)
                lhs[0:1, lane] = w_re[i:i + 1]
                lhs[1:2, lane] = w_im[i:i + 1]
        for begin, size in pieces[c]:
            at = slice(begin, begin + size)
            w_re, w_im = lhs[0:1, at], lhs[1:2, at]
            rows_of = [
                jnp.concatenate([w_re, w_im], axis=0).astype(jnp.bfloat16),
                jnp.concatenate([w_im, -w_re], axis=0).astype(jnp.bfloat16),
            ]
            for p in range(2):
                beam_copies[begin, p].wait()
                term = jnp.dot(rows_of[p], beam_v[p, at, :], preferred_element_type=jnp.float32)
                total = term if total is None else total + term

    width = beam.shape[3] // n_bl
    for d in range(n_bl):
        share[d, :, 0, 0:width] = total[:, d * width:(d + 1) * width]
    bl_copies = []
    for k in range(1, n_bl):
        copy = pltpu.make_async_remote_copy(
            src_ref=share.at[bl_peers[k]], dst_ref=out.at[my_bl],
            send_sem=bl_send.at[k], recv_sem=bl_recv.at[k],
            device_id={"bl": bl_peers[k]}, device_id_type=MESH,
        )
        copy.start()
        bl_copies.append(copy)
    out[my_bl] = share[my_bl]
    for copy in near_copies.values():
        copy.wait_send()
    for copy in far_copies.values():
        copy.wait_send()
    for copy in bl_copies:
        copy.wait_send()
    for copy in bl_copies:
        copy.wait_recv()


def per_device(n_ma, n_bl, visibilities, beam_blocks, feed_pairs, feed_gains, m_order):
    _, rows, local_times = visibilities.shape
    width = beam_blocks.shape[3]
    assert m_order.shape[0] == n_ma and beam_blocks.shape[0] == 1 and n_ma % 16 == 0
    cols = rows // LANES
    rem = rows - cols * LANES
    per = cols // CHUNKS
    assert per * LANES % PIECE == 0 and cols % CHUNKS == 0 and (2 * per) % 16 == 0 and 0 < 2 * rem <= LANES
    chips = n_ma // 2
    share_width = width // n_bl
    share_pad = -(-share_width // LANES) * LANES
    feeds = feed_gains.shape[1]
    f32, bf16 = jnp.float32, jnp.bfloat16
    dma = pltpu.SemaphoreType.DMA
    parts = pl.pallas_call(
        functools.partial(kernel, n_ma, n_bl),
        out_shape=jax.ShapeDtypeStruct((n_bl, 2, 1, share_pad), f32),
        in_specs=[pl.BlockSpec(memory_space=pl.ANY)] * 5,
        out_specs=pl.BlockSpec(memory_space=pltpu.VMEM),
        scratch_shapes=[
            pltpu.VMEM((2, rows, local_times), bf16),
            pltpu.VMEM((2, rows, width), bf16),
            pltpu.VMEM((2, rows), jnp.int32),
            pltpu.VMEM((2, feeds), f32),
            pltpu.SMEM((n_ma,), jnp.int32),
            pltpu.VMEM((CHUNKS, 2, chips * 2 * per, LANES), f32),
            pltpu.VMEM((CHUNKS, chips * 2 * per, LANES), f32),
            pltpu.VMEM((CHUNKS, chips, 2 * per, LANES), bf16),
            pltpu.VMEM((CHUNKS, chips, 2 * per, LANES), bf16),
            pltpu.VMEM((2, chips, 1, LANES), f32),
            pltpu.VMEM((chips, 1, LANES), f32),
            pltpu.VMEM((chips, 1, LANES), f32),
            pltpu.VMEM((chips, 1, LANES), f32),
            pltpu.VMEM((2 * feeds // LANES, LANES), f32),
            pltpu.VMEM((2, cols, LANES), f32),
            pltpu.VMEM((8, rows), f32),
            pltpu.VMEM((n_bl, 2, 1, share_pad), f32),
            dma((2 * (cols * LANES // PIECE + 1),)),
            dma((2 * (cols * LANES // PIECE + 1),)),
            dma((3,)),
            dma((CHUNKS + 1,)),
            dma((CHUNKS + 1,)),
            dma((CHUNKS + 1, chips)),
            dma((CHUNKS + 1, chips)),
            dma((n_bl,)),
            dma((n_bl,)),
        ],
        compiler_params=pltpu.CompilerParams(
            collective_id=0, has_side_effects=True, vmem_limit_bytes=VMEM_LIMIT
        ),
        cost_estimate=pl.CostEstimate(
            flops=2 * rows * (2 * local_times * 2 * n_ma + 4 * width),
            bytes_accessed=4 * rows * (local_times + width),
            transcendentals=0,
        ),
    )(visibilities, beam_blocks, feed_pairs.T, feed_gains, m_order)
    result = parts[0, :, :, :share_width]
    for d in range(1, n_bl):
        result = result + parts[d, :, :, :share_width]
    return result


def solution(mesh):
    return jax.shard_map(
        functools.partial(per_device, mesh.shape["ma"], mesh.shape["bl"]),
        mesh=mesh,
        in_specs=(P(None, "bl", "ma"), P("ma", None, "bl", None), P("bl", None), P(), P()),
        out_specs=P(None, "ma", "bl"),
        check_vma=False,
    )
```

```python
import functools

import jax
import jax.numpy as jnp
import numpy as np
from jax import lax
from jax.experimental import pallas as pl
from jax.experimental.pallas import tpu as pltpu
from jax.sharding import PartitionSpec as P

NT = 8192
LANES = 128
CHUNKS = 2
PIECE = 1024
VMEM_LIMIT = 55216 * 2**10
MESH = pl.DeviceIdType.MESH


def trig(k):
    quarter = NT // 4
    turn = (k + quarter // 2) // quarter
    x = (k - turn * quarter).astype(jnp.float32) * np.float32(2.0 * np.pi / NT)
    y = x * x
    sin_x = x * (1.0 + y * (-1.0 / 6 + y * (1.0 / 120 + y * (-1.0 / 5040 + y * (1.0 / 362880)))))
    cos_x = 1.0 + y * (-0.5 + y * (1.0 / 24 + y * (-1.0 / 720 + y * (1.0 / 40320))))
    odd = (turn & 1) == 1
    cos_k = jnp.where(odd, sin_x, cos_x)
    sin_k = jnp.where(odd, cos_x, sin_x)
    cos_k = jnp.where(((turn + 1) & 2) == 2, -cos_k, cos_k)
    sin_k = jnp.where((turn & 2) == 2, -sin_k, sin_k)
    return cos_k, sin_k


def kernel(
    n_ma, n_bl, vis, beam, pairs, gains, order, out,
    vis_v, beam_v, pairs_v, gains_v, order_s,
    sums, near, part, got, rem_sums, rem_near, rem_part, rem_got, table, factor, lhs, share,
    vis_sem, beam_sem, small_sem, near_send, near_recv, send_sem, recv_sem, bl_send, bl_recv,
):
    me = lax.axis_index("ma")
    my_bl = lax.axis_index("bl")
    rows = vis.shape[1]
    local_times = vis.shape[2]
    cols = rows // LANES
    rem = rows - cols * LANES
    per = cols // CHUNKS
    chips = n_ma // 2
    chip = me // 2
    core = lax.rem(me, 2)
    other = 1 - core
    sibling = chip * 2 + other
    far = [lax.rem(chip + k, chips) for k in range(chips)]
    far_order = sorted(range(1, chips), key=lambda k: abs(k - chips // 2))

    order_copy = pltpu.make_async_copy(order, order_s, small_sem.at[0])
    order_copy.start()
    spans = [(c * per * LANES, per * LANES) for c in range(CHUNKS)] + [(cols * LANES, rem)]
    load_order = [0, CHUNKS] + list(range(1, CHUNKS))
    pieces = {}
    for c in load_order:
        start, size = spans[c]
        pieces[c] = [(at, min(PIECE, start + size - at)) for at in range(start, start + size, PIECE)]
    vis_copies, beam_copies = {}, {}
    slot = 0
    for c in load_order:
        for at, size in pieces[c]:
            for p in range(2):
                piece = pl.ds(at, size)
                vis_copies[at, p] = pltpu.make_async_copy(vis.at[p, piece], vis_v.at[p, piece], vis_sem.at[slot])
                vis_copies[at, p].start()
                beam_copies[at, p] = pltpu.make_async_copy(
                    beam.at[0, p, piece], beam_v.at[p, piece], beam_sem.at[slot]
                )
                slot += 1
    pairs_copy = pltpu.make_async_copy(pairs, pairs_v, small_sem.at[1])
    pairs_copy.start()
    gains_copy = pltpu.make_async_copy(gains, gains_v, small_sem.at[2])
    gains_copy.start()

    barrier = pltpu.get_barrier_semaphore()
    pl.semaphore_signal(barrier, inc=1, device_id={"ma": sibling}, device_id_type=MESH)
    for k in range(1, chips):
        pl.semaphore_signal(barrier, inc=1, device_id={"ma": far[k] * 2 + core}, device_id_type=MESH)
    bl_peers = [lax.rem(my_bl + k, n_bl) for k in range(n_bl)]
    for k in range(1, n_bl):
        pl.semaphore_signal(barrier, inc=1, device_id={"bl": bl_peers[k]}, device_id_type=MESH)

    order_copy.wait()
    row_of = lax.broadcasted_iota(jnp.int32, (n_ma, LANES), 0)
    m_value = jnp.zeros((n_ma, LANES), jnp.int32)
    for j in range(n_ma):
        m_value = jnp.where(row_of == (j % 2) * chips + j // 2, order_s[j] - n_ma // 2, m_value)
    left, right = [], []
    for block in range(local_times // LANES):
        time = me * local_times + block * LANES + lax.broadcasted_iota(jnp.int32, (n_ma, LANES), 1)
        cos_k, sin_k = trig((time * m_value) & (NT - 1))
        scale = np.float32(1.0 / np.sqrt(np.float32(NT)))
        cos_k, sin_k = cos_k * scale, sin_k * scale
        left.append(jnp.concatenate([cos_k, -sin_k], axis=0).T.astype(jnp.bfloat16))
        right.append(jnp.concatenate([sin_k, cos_k], axis=0).T.astype(jnp.bfloat16))
    left = jnp.concatenate(left, axis=0)
    right = jnp.concatenate(right, axis=0)

    def transform(start, size):
        flat = jnp.dot(vis_v[0, start:start + size, :], left, preferred_element_type=jnp.float32)
        flat = flat + jnp.dot(vis_v[1, start:start + size, :], right, preferred_element_type=jnp.float32)
        return flat.T

    near_copies = {}

    def to_sibling(c, source, target):
        near_copies[c] = pltpu.make_async_remote_copy(
            src_ref=source, dst_ref=target, send_sem=near_send.at[c], recv_sem=near_recv.at[c],
            device_id={"ma": sibling}, device_id_type=MESH,
        )
        near_copies[c].start()

    def start_beam(which):
        for c in which:
            for at, _ in pieces[c]:
                for p in range(2):
                    beam_copies[at, p].start()

    far_copies = {}

    def to_far(c):
        near_copies[c].wait_recv()
        if c == CHUNKS:
            rem_part[...] = rem_sums[core] + rem_near[...]
        else:
            both = sums[c, core] + near[c]
            sums[c, core] = both
            part[c] = both.astype(jnp.bfloat16).reshape(chips, 2 * per, LANES)
        for k in far_order:
            source = rem_part.at[far[k]] if c == CHUNKS else part.at[c, far[k]]
            target = rem_got.at[chip] if c == CHUNKS else got.at[c, chip]
            far_copies[c, k] = pltpu.make_async_remote_copy(
                src_ref=source, dst_ref=target, send_sem=send_sem.at[c, k], recv_sem=recv_sem.at[c, k],
                device_id={"ma": far[k] * 2 + core}, device_id_type=MESH,
            )
            far_copies[c, k].start()

    for c in load_order:
        for number, (at, size) in enumerate(pieces[c]):
            for p in range(2):
                vis_copies[at, p].wait()
            if c == load_order[-1] and number == 0:
                start_beam(load_order[:-1])
            if c == CHUNKS:
                flat = transform(at, size)
                wide = jnp.concatenate(
                    [flat[:n_ma], flat[n_ma:], jnp.zeros((n_ma, LANES - 2 * rem), jnp.float32)], axis=1
                )
                for j in range(n_ma):
                    rem_sums[j // chips, j % chips] = wide[j:j + 1, :]
                continue
            for begin in range(at, at + size, 2 * LANES):
                flat = transform(begin, 2 * LANES)
                for u in range(2):
                    row = (begin - spans[c][0]) // LANES + u
                    for p in range(2):
                        for g in range(2):
                            from_row = p * n_ma + g * chips
                            sums[c, g, pl.ds(p * per + row, chips, stride=2 * per), :] = (
                                flat[from_row:from_row + chips, u * LANES:(u + 1) * LANES]
                            )
        if c == 0:
            pl.semaphore_wait(barrier, 1 + chips - 1 + n_bl - 1)
        if c == CHUNKS:
            to_sibling(c, rem_sums.at[other], rem_near)
        else:
            to_sibling(c, sums.at[c, other], near.at[c])

    for c in load_order[:-1]:
        to_far(c)
    start_beam(load_order[-1:])

    pairs_copy.wait()
    gains_copy.wait()
    high = gains.shape[1] // LANES
    for comp in range(2):
        for h in range(high):
            table[comp * high + h:comp * high + h + 1, :] = gains_v[comp:comp + 1, h * LANES:(h + 1) * LANES]
    whole = table[...]
    first = whole.astype(jnp.bfloat16)
    rest = whole - first.astype(jnp.float32)
    second = rest.astype(jnp.bfloat16)
    third = (rest - second.astype(jnp.float32)).astype(jnp.bfloat16)
    thirds = jnp.concatenate([first, second, third], axis=0)

    def gain_of(feed, start, size):
        index = pairs_v[feed:feed + 1, start:start + size]
        low = lax.broadcasted_iota(jnp.int32, (LANES, size), 0)
        hot = jnp.where(low == (index & (LANES - 1)), 1.0, 0.0).astype(jnp.bfloat16)
        picked = jnp.dot(thirds, hot, preferred_element_type=jnp.float32)
        picked = picked[:2 * high] + picked[2 * high:4 * high] + picked[4 * high:]
        mask = lax.broadcasted_iota(jnp.int32, (high, size), 0) == index // LANES
        re = jnp.sum(jnp.where(mask, picked[:high], 0.0), axis=0, keepdims=True)
        im = jnp.sum(jnp.where(mask, picked[high:], 0.0), axis=0, keepdims=True)
        return re, im

    def factor_of(start, size):
        a_re, a_im = gain_of(0, start, size)
        b_re, b_im = gain_of(1, start, size)
        return a_re * b_re + a_im * b_im, a_im * b_re - a_re * b_im

    for i in range(0, cols, 2):
        f_re, f_im = factor_of(i * LANES, 2 * LANES)
        for u in range(2):
            factor[0, i + u:i + u + 1, :] = f_re[:, u * LANES:(u + 1) * LANES]
            factor[1, i + u:i + u + 1, :] = f_im[:, u * LANES:(u + 1) * LANES]
    rem_re, rem_im = factor_of(*spans[CHUNKS])

    to_far(load_order[-1])

    def weigh(s_re, s_im, f_re, f_im):
        s_re = s_re.astype(jnp.bfloat16).astype(jnp.float32)
        s_im = s_im.astype(jnp.bfloat16).astype(jnp.float32)
        return s_re * f_re - s_im * f_im, s_re * f_im + s_im * f_re

    full = beam.shape[3]
    split = (full + 255) // 256 // 2 * 256
    tail_total = jnp.zeros((2, full), jnp.float32)
    low_total = jnp.zeros((2, split), jnp.float32)
    high_re = jnp.zeros((16, full - split), jnp.float32)
    high_im = jnp.zeros((16, full - split), jnp.float32)
    for c in load_order:
        for k in far_order:
            far_copies[c, k].wait_recv()
        start, size = spans[c]
        at = slice(start, start + size)
        if c == CHUNKS:
            tail = rem_part[chip]
            for k in far_order:
                tail = tail + rem_got[far[k]]
            w_re, w_im = weigh(tail[:, :rem], tail[:, rem:2 * rem], rem_re, rem_im)
            lhs[0:1, at] = w_re
            lhs[1:2, at] = w_im
        else:
            mine = pl.multiple_of(chip * 2 * per, 2 * per)
            spectra = sums[c, core, pl.ds(mine, 2 * per), :]
            for k in far_order:
                spectra = spectra + got[c, far[k]].astype(jnp.float32)
            w_re, w_im = weigh(
                spectra[:per], spectra[per:], factor[0, c * per:(c + 1) * per], factor[1, c * per:(c + 1) * per]
            )
            for i in range(per):
                lane = slice(start + i * LANES, start + (i + 1) * LANES)
                lhs[0:1, lane] = w_re[i:i + 1]
                lhs[1:2, lane] = w_im[i:i + 1]
        columns = [w.astype(jnp.bfloat16).astype(jnp.float32).T for w in (w_re, w_im)] if c < CHUNKS else None
        for begin, size in pieces[c]:
            at = slice(begin, begin + size)
            w_re, w_im = lhs[0:1, at], lhs[1:2, at]
            rows_of = [
                jnp.concatenate([w_re, w_im], axis=0).astype(jnp.bfloat16),
                jnp.concatenate([w_im, -w_re], axis=0).astype(jnp.bfloat16),
            ]
            for p in range(2):
                beam_copies[begin, p].wait()
            if c == CHUNKS:
                for p in range(2):
                    tail_total = tail_total + jnp.dot(
                        rows_of[p], beam_v[p, at, :], preferred_element_type=jnp.float32
                    )
                continue
            for p in range(2):
                low_total = low_total + jnp.dot(
                    rows_of[p], beam_v[p, at, :split], preferred_element_type=jnp.float32
                )
            for row in range(begin, begin + size, 16):
                col = (row - start) // LANES
                r = (row - start) % LANES
                v_re = columns[0][r:r + 16, col:col + 1]
                v_im = columns[1][r:r + 16, col:col + 1]
                b_re = beam_v[0, row:row + 16, split:].astype(jnp.float32)
                b_im = beam_v[1, row:row + 16, split:].astype(jnp.float32)
                high_re = high_re + (b_re * v_re + b_im * v_im)
                high_im = high_im + (b_re * v_im - b_im * v_re)

    high = jnp.concatenate(
        [jnp.sum(high_re, axis=0, keepdims=True), jnp.sum(high_im, axis=0, keepdims=True)], axis=0
    )
    total = tail_total + jnp.concatenate([low_total, high], axis=1)
    width = beam.shape[3] // n_bl
    for d in range(n_bl):
        share[d, :, 0, 0:width] = total[:, d * width:(d + 1) * width]
    bl_copies = []
    for k in range(1, n_bl):
        copy = pltpu.make_async_remote_copy(
            src_ref=share.at[bl_peers[k]], dst_ref=out.at[my_bl],
            send_sem=bl_send.at[k], recv_sem=bl_recv.at[k],
            device_id={"bl": bl_peers[k]}, device_id_type=MESH,
        )
        copy.start()
        bl_copies.append(copy)
    out[my_bl] = share[my_bl]
    for copy in near_copies.values():
        copy.wait_send()
    for copy in far_copies.values():
        copy.wait_send()
    for copy in bl_copies:
        copy.wait_send()
    for copy in bl_copies:
        copy.wait_recv()


def per_device(n_ma, n_bl, visibilities, beam_blocks, feed_pairs, feed_gains, m_order):
    _, rows, local_times = visibilities.shape
    width = beam_blocks.shape[3]
    assert m_order.shape[0] == n_ma and beam_blocks.shape[0] == 1 and n_ma % 16 == 0
    cols = rows // LANES
    rem = rows - cols * LANES
    per = cols // CHUNKS
    assert per * LANES % PIECE == 0 and cols % CHUNKS == 0 and (2 * per) % 16 == 0 and 0 < 2 * rem <= LANES
    chips = n_ma // 2
    share_width = width // n_bl
    share_pad = -(-share_width // LANES) * LANES
    feeds = feed_gains.shape[1]
    f32, bf16 = jnp.float32, jnp.bfloat16
    dma = pltpu.SemaphoreType.DMA
    parts = pl.pallas_call(
        functools.partial(kernel, n_ma, n_bl),
        out_shape=jax.ShapeDtypeStruct((n_bl, 2, 1, share_pad), f32),
        in_specs=[pl.BlockSpec(memory_space=pl.ANY)] * 5,
        out_specs=pl.BlockSpec(memory_space=pltpu.VMEM),
        scratch_shapes=[
            pltpu.VMEM((2, rows, local_times), bf16),
            pltpu.VMEM((2, rows, width), bf16),
            pltpu.VMEM((2, rows), jnp.int32),
            pltpu.VMEM((2, feeds), f32),
            pltpu.SMEM((n_ma,), jnp.int32),
            pltpu.VMEM((CHUNKS, 2, chips * 2 * per, LANES), f32),
            pltpu.VMEM((CHUNKS, chips * 2 * per, LANES), f32),
            pltpu.VMEM((CHUNKS, chips, 2 * per, LANES), bf16),
            pltpu.VMEM((CHUNKS, chips, 2 * per, LANES), bf16),
            pltpu.VMEM((2, chips, 1, LANES), f32),
            pltpu.VMEM((chips, 1, LANES), f32),
            pltpu.VMEM((chips, 1, LANES), f32),
            pltpu.VMEM((chips, 1, LANES), f32),
            pltpu.VMEM((2 * feeds // LANES, LANES), f32),
            pltpu.VMEM((2, cols, LANES), f32),
            pltpu.VMEM((8, rows), f32),
            pltpu.VMEM((n_bl, 2, 1, share_pad), f32),
            dma((2 * (cols * LANES // PIECE + 1),)),
            dma((2 * (cols * LANES // PIECE + 1),)),
            dma((3,)),
            dma((CHUNKS + 1,)),
            dma((CHUNKS + 1,)),
            dma((CHUNKS + 1, chips)),
            dma((CHUNKS + 1, chips)),
            dma((n_bl,)),
            dma((n_bl,)),
        ],
        compiler_params=pltpu.CompilerParams(
            collective_id=0, has_side_effects=True, vmem_limit_bytes=VMEM_LIMIT
        ),
        cost_estimate=pl.CostEstimate(
            flops=2 * rows * (2 * local_times * 2 * n_ma + 4 * width),
            bytes_accessed=4 * rows * (local_times + width),
            transcendentals=0,
        ),
    )(visibilities, beam_blocks, feed_pairs.T, feed_gains, m_order)
    result = parts[0, :, :, :share_width]
    for d in range(1, n_bl):
        result = result + parts[d, :, :, :share_width]
    return result


def solution(mesh):
    return jax.shard_map(
        functools.partial(per_device, mesh.shape["ma"], mesh.shape["bl"]),
        mesh=mesh,
        in_specs=(P(None, "bl", "ma"), P("ma", None, "bl", None), P("bl", None), P(), P()),
        out_specs=P(None, "ma", "bl"),
        check_vma=False,
    )
```
